32 devices in a mesh: section: 4 (over z), expert: 8 (over y, x, core).
Axes of the slice: x: 2, y: 2, z: 4, core: 2. Of those that a mesh axis runs over, the one named last changes fastest.
Arguments:
- acts: bfloat16 [4, 2048, 2048], P('section', 'expert'), may hold values from -6 to 6
- expert_ids: int32 [4, 2048, 2], P('section', 'expert'), may hold values from 0 to 7, all different within a row; in each aligned block of 256 rows (0 to 255, 256 to 511, ..., all dimensions but the last counted through in order) at most 96 rows name the same one
- router: bfloat16 [4, 2048, 8], P('section'), may hold values from -0.125 to 0.125
- skip_gain: float32 [4, 2048], P('section'), may hold values from 0.5 to 1.5
- skip_rows: bfloat16 [4, 2048, 2048], P('section', 'expert'), may hold values from -6 to 6
- w_in: bfloat16 [4, 8, 2048, 1024], P('section', 'expert'), may hold values from -0.125 to 0.125
- w_out: bfloat16 [4, 8, 1024, 2048], P('section', 'expert'), may hold values from -0.1875 to 0.1875
Outputs:
- handed: bfloat16 [4, 2048, 2048], P('section', 'expert')
- mirrored: bfloat16 [4, 2048, 2048], P('section', 'expert')
The draws below stay inside these ranges and needn't reach their ends.
Inputs may be any that keep to these rules, and one draw needn't show every extreme that they name: `expert_ids`: each token names 2 different experts. Among the 256 tokens of one group no expert is named more than 96 times, a bound that some block reaches.
All inputs are finite; a program needn't handle non-finite values.
Results may differ from the reference program's by a relative error of at most 0.0041.
Values may be sent and summed in bfloat16 or wider, within the bound.
No kernel may reach another device: no remote copies, remote signals or barrier semaphores. Data moves between devices by JAX's collectives and lax.ppermute only.
A program may use at most 64 MiB of HBM per device.

```python
import math
import jax
import jax.numpy as jnp
import numpy as np
from jax import lax

D = 2048
FF = 1024
TOP = 2
TOK_DEV = 256
EXPERTS = 8
TOKENS = 2048
SECTIONS = 4
CAP = 96
N_EXPERT = 8


def block_scale(key, extent, pieces, low, largest):
    factor_of = 1.0
    for axis_at, blocks in pieces:
        steps = jax.random.uniform(jax.random.fold_in(jax.random.fold_in(key, 6), axis_at), (blocks,), jnp.float32, low / len(pieces), largest / len(pieces))
        factor_of = factor_of * jnp.repeat(jnp.exp(steps), extent[axis_at] // blocks).reshape((-1,) + (1,) * (len(extent) - 1 - axis_at))
    return factor_of


def routed_block(stream_key, own, number, rows, number_of, top, bound, skew):
    sequence = jax.random.permutation(stream_key, number_of)
    heavy_load, usual = portions_of(number_of, rows * top, bound, skew, True), portions_of(number_of, rows * top, bound, skew, False)
    places = jnp.arange(number_of)

    def named(tallies, rotation):
        used = int((tallies > 0).sum())
        fixed = max(1, used // 4)
        shifted = fixed + (places - fixed + rotation * (used - fixed)) % max(1, number_of - fixed)
        return jnp.zeros((number_of,), jnp.int32).at[sequence[jnp.where(places < fixed, places, shifted)]].set(jnp.asarray(tallies, jnp.int32))

    tallies = jnp.where(number % 4 == 0, named(heavy_load, number // 4), named(usual, number - number // 4 - 1))
    mixed = jax.random.permutation(jax.random.fold_in(own, 3), number_of)
    source_of, sink = mixed[0:number_of // 2 * 2:2], mixed[1:number_of // 2 * 2:2]
    slack = jnp.minimum(tallies[source_of] - 1, bound - tallies[sink]) // 2
    slack = jnp.where((source_of == sequence[0]) | (sink == sequence[0]) | (tallies[sink] == 0), 0, jnp.maximum(slack, 0))
    shifted = jax.random.randint(jax.random.fold_in(own, 4), (number_of // 2,), 0, 1 << 20) % (slack + 1)
    tallies = tallies.at[source_of].add(-shifted).at[sink].add(shifted)
    items = jnp.searchsorted(jnp.cumsum(tallies), jnp.arange(rows * top), side="right").astype(jnp.int32)
    listing = items.reshape(top, rows).T
    listing = listing[jax.random.permutation(jax.random.fold_in(own, 1), rows)]
    rotation = jax.random.randint(jax.random.fold_in(own, 2), (rows, 1), 0, top)
    return jnp.take_along_axis(listing, (jnp.arange(top)[None, :] + rotation) % top, axis=1)


def portions_of(number_of, total, most, slope, full):
    portions = [(1 << 20) // math.isqrt(rank ** slope) + 1 for rank in range(1, number_of + 1)]
    largest = most if full else min(most, max(-(-total // number_of), total * portions[0] // sum(portions)))
    least = 1 if total - largest >= number_of - 1 else 0
    given, surplus = [largest] + [least] * (number_of - 1), total - largest - least * (number_of - 1)
    while surplus > 0:
        candidates = [i for i in range(1, number_of) if given[i] < largest] or [i for i in range(1, number_of) if given[i] < most]
        mass, left = sum([portions[i] for i in candidates]), surplus
        for i in candidates:
            extra = min(most - given[i], max(1, left * portions[i] // mass), surplus)
            given[i] = given[i] + extra
            surplus = surplus - extra
    return np.array(given)


def noise(key, dims, width, bound, shards=(), held_as=jnp.bfloat16):
    result = width * jax.random.normal(key, dims, jnp.float32)
    if shards:
        result = result * block_scale(key, dims, shards, -0.22, 0.18)
    return jnp.clip(result, -bound, bound).astype(held_as)


def setup_inputs(seed: int = 0) -> dict:
    seeds = jax.random.split(jax.random.key(seed), 8)
    acts = noise(seeds[0], (SECTIONS, TOKENS, D), 1.0, 6.0, ((0, 4), (1, 8)))
    expert_ids_keys = jax.random.split(jax.random.fold_in(seeds[1], 1), SECTIONS * TOKENS // TOK_DEV)
    expert_ids_turns = jax.random.permutation(jax.random.fold_in(seeds[1], 3), SECTIONS * TOKENS // TOK_DEV)
    expert_ids = jax.vmap(lambda own, number: routed_block(jax.random.fold_in(seeds[1], 2), own, number, TOK_DEV, EXPERTS, TOP, CAP, 2))(expert_ids_keys, expert_ids_turns).reshape((SECTIONS, TOKENS, TOP))
    router = noise(seeds[2], (SECTIONS, D, EXPERTS), D ** -0.5, 0.125, ((0, 4),))
    skip_gain = jnp.clip(0.5 + 1.0 * jax.random.uniform(seeds[3], (SECTIONS, D), jnp.float32) ** block_scale(seeds[3], (SECTIONS, D), ((0, 4),), -0.2, 0.2), 0.5, 1.5)
    skip_rows = noise(seeds[4], (SECTIONS, TOKENS, D), 1.0, 6.0, ((0, 4), (1, 8)))
    w_in = noise(seeds[5], (SECTIONS, EXPERTS, D, FF), D ** -0.5, 0.125, ((0, 4), (1, 8)))
    w_out = noise(seeds[6], (SECTIONS, EXPERTS, FF, D), FF ** -0.5, 0.1875, ((0, 4), (1, 8)))
    return dict(acts=acts, expert_ids=expert_ids, router=router, skip_gain=skip_gain, skip_rows=skip_rows, w_in=w_in, w_out=w_out)


def rms(values):
    return values * lax.rsqrt(lax.optimization_barrier(jnp.mean(values * values, axis=-1, keepdims=True)) + 1e-06)

def slots_of(group_ids):
    flat = group_ids.reshape(-1)
    onehot = (flat[:, None] == jnp.arange(EXPERTS, dtype=jnp.int32)[None, :]).astype(jnp.int32)
    before = jnp.cumsum(onehot, axis=0) - onehot
    return lax.optimization_barrier(jnp.sum(before * onehot, axis=1)).astype(jnp.int32).reshape(group_ids.shape)

def expert_apply(operands):
    rows, first, second = operands
    hidden = jax.nn.gelu(jnp.dot(rows, first, preferred_element_type=jnp.float32), approximate=True).astype(jnp.bfloat16)
    return jnp.dot(hidden, second, preferred_element_type=jnp.float32).astype(jnp.bfloat16)

def reference(acts, expert_ids, router, skip_gain, skip_rows, w_in, w_out):
    outputs = []
    for section in range(SECTIONS):
        h_rows = acts[section].astype(jnp.float32)
        if section >= SECTIONS // 2:
            h_rows = h_rows + skip_gain[section][None, :] * rms(skip_rows[section].astype(jnp.float32))
        normed = rms(h_rows).astype(jnp.bfloat16)
        logits = jnp.dot(normed, router[section], preferred_element_type=jnp.float32)
        chosen = jnp.take_along_axis(logits, expert_ids[section], axis=1)
        gates = jax.nn.softmax(chosen, axis=-1)
        groups = expert_ids[section].reshape(N_EXPERT, TOK_DEV, TOP)
        slot = jax.vmap(slots_of)(groups).reshape(TOKENS, TOP)
        source = (jnp.arange(TOKENS, dtype=jnp.int32) // TOK_DEV)[:, None]
        row_pos = (source * CAP + slot).reshape(-1).astype(jnp.int32)
        flat_ids = expert_ids[section].reshape(-1).astype(jnp.int32)
        repeated = jnp.repeat(normed, TOP, axis=0)
        buffer = jnp.zeros((EXPERTS, N_EXPERT * CAP, D), jnp.bfloat16).at[flat_ids, row_pos].set(repeated)
        expert_out = lax.map(expert_apply, (buffer, w_in[section], w_out[section]))
        fetched = expert_out[flat_ids, row_pos].reshape(TOKENS, TOP, D).astype(jnp.float32)
        combined = lax.optimization_barrier(jnp.sum(gates[:, :, None] * fetched, axis=1))
        outputs.append((h_rows + combined).astype(jnp.bfloat16))
    stacked = jnp.stack(outputs, axis=0)
    handed = jnp.roll(stacked, 1, axis=0)
    mirrored = stacked[::-1]
    return (handed, mirrored)
```

```python
import jax
import jax.numpy as jnp
from jax import lax
from jax.experimental import pallas as pl
from jax.experimental.pallas import tpu as pltpu
from jax.sharding import PartitionSpec as P

OUT_CHUNKS = 4
IN_CHUNKS = 1


def inverse_rms(values):
    return lax.rsqrt(jnp.mean(values * values, axis=-1, keepdims=True) + 1e-06)


def slot_table(ids, experts, capacity):
    tokens = ids.shape[0]
    rows = experts * capacity
    named = jnp.zeros((tokens, experts), jnp.float32)
    lane = lax.broadcasted_iota(jnp.int32, (tokens, experts), 1)
    for k in range(ids.shape[1]):
        named = named + jnp.where(ids[:, k : k + 1] == lane, 1.0, 0.0)
    before = lax.broadcasted_iota(jnp.int32, (tokens, tokens), 0)
    after = lax.broadcasted_iota(jnp.int32, (tokens, tokens), 1)
    weight = jnp.where(before < after, 1.0, jnp.where(before == after, 512.0, 0.0))
    tally = lax.dot_general(
        named.astype(jnp.bfloat16),
        weight.astype(jnp.bfloat16),
        (((0,), (0,)), ((), ())),
        preferred_element_type=jnp.float32,
    )
    slot = jnp.where(tally >= 512.0, tally - 512.0, -1.0)
    row = lax.broadcasted_iota(jnp.int32, (rows, experts), 0)
    column = lax.broadcasted_iota(jnp.int32, (rows, experts), 1)
    low = column * capacity
    spread = jnp.where((row >= low) & (row < low + capacity), 1.0, 0.0)
    wanted = jnp.dot(
        spread.astype(jnp.bfloat16), slot.astype(jnp.bfloat16), preferred_element_type=jnp.float32
    )
    first = jnp.sum(spread * low.astype(jnp.float32), axis=1, keepdims=True)
    place = lax.broadcasted_iota(jnp.int32, (rows, 1), 0).astype(jnp.float32) - first
    return wanted == place, spread, named


def dispatch_kernel(experts, capacity, late_ref, acts_ref, ids_ref, gain_ref, skip_ref, buffer_ref, h_ref, normed_ref):
    skip = skip_ref[...].astype(jnp.float32)
    term = gain_ref[...] * (skip * inverse_rms(skip))
    h = acts_ref[...].astype(jnp.float32) + jnp.where(late_ref[0] > 0, term, jnp.zeros_like(term))
    h_ref[...] = h
    normed = (h * inverse_rms(h)).astype(jnp.bfloat16)
    normed_ref[...] = normed
    taken, _, _ = slot_table(ids_ref[...], experts, capacity)
    pick = jnp.where(taken, 1.0, 0.0).astype(jnp.bfloat16)
    buffer_ref[...] = jnp.dot(pick, normed, preferred_element_type=jnp.float32).astype(jnp.bfloat16)


def gate_kernel(experts, capacity, normed_ref, ids_ref, router_ref, mix_ref):
    logits = jnp.dot(normed_ref[...], router_ref[...], preferred_element_type=jnp.float32)
    taken, spread, named = slot_table(ids_ref[...], experts, capacity)
    chosen = named > 0.0
    peak = jnp.max(jnp.where(chosen, logits, -jnp.inf), axis=1, keepdims=True)
    mass = jnp.where(chosen, jnp.exp(logits - peak), 0.0)
    gates = mass / jnp.sum(mass, axis=1, keepdims=True)
    wide = lax.dot_general(
        spread.astype(jnp.bfloat16),
        gates.astype(jnp.bfloat16),
        (((1,), (1,)), ((), ())),
        preferred_element_type=jnp.float32,
    )
    mix_ref[...] = jnp.where(taken, wide, 0.0).T.astype(jnp.bfloat16)


def local(acts, expert_ids, router, skip_gain, skip_rows, w_in, w_out):
    section_pos = lax.axis_index("section")
    sections = lax.axis_size("section")
    tokens, width = acts.shape[1:]
    topk = expert_ids.shape[2]
    experts = router.shape[2]
    capacity = 3 * tokens * topk // (2 * experts)
    rows = experts * capacity
    late = (section_pos >= sections // 2).astype(jnp.int32).reshape(1)
    ids = expert_ids[0]
    whole = pl.BlockSpec(memory_space=pltpu.VMEM)
    buffer, h_rows, normed = pl.pallas_call(
        lambda *refs: dispatch_kernel(experts, capacity, *refs),
        out_shape=(
            jax.ShapeDtypeStruct((rows, width), jnp.bfloat16),
            jax.ShapeDtypeStruct((tokens, width), jnp.float32),
            jax.ShapeDtypeStruct((tokens, width), jnp.bfloat16),
        ),
        in_specs=[pl.BlockSpec(memory_space=pltpu.SMEM)] + [whole] * 4,
        out_specs=(whole,) * 3,
        compiler_params=pltpu.CompilerParams(vmem_limit_bytes=48 * 2**20),
        name="dispatch",
    )(late, acts[0], ids, skip_gain, skip_rows[0])

    def exchange(block):
        return lax.all_to_all(block, "expert", split_axis=0, concat_axis=0, tiled=True)

    send = buffer.reshape(experts, capacity, width)
    step = width // IN_CHUNKS
    summed = None
    for c in range(IN_CHUNKS):
        part = exchange(send[:, :, c * step : (c + 1) * step]).reshape(rows, step)
        term = jnp.dot(part, w_in[0, 0, c * step : (c + 1) * step], preferred_element_type=jnp.float32)
        summed = term if summed is None else summed + term
    hidden = jax.nn.gelu(summed, approximate=True).astype(jnp.bfloat16)

    mix = pl.pallas_call(
        lambda *refs: gate_kernel(experts, capacity, *refs),
        out_shape=jax.ShapeDtypeStruct((tokens, rows), jnp.bfloat16),
        in_specs=[whole] * 3,
        out_specs=whole,
        compiler_params=pltpu.CompilerParams(vmem_limit_bytes=48 * 2**20),
        name="gates",
    )(normed, ids, router[0])

    mirror = [(s, sections - 1 - s) for s in range(sections)]
    same = [s for s in range(sections) if (s - 1) % sections == sections - 1 - s]
    onward = [((s - 1) % sections, s) for s in range(sections) if s not in same]
    shared = jnp.zeros((), jnp.bool_)
    for s in same:
        shared = shared | (section_pos == s)
    step = width // OUT_CHUNKS
    mirrored, handed = [], []
    for c in range(OUT_CHUNKS):
        columns = slice(c * step, (c + 1) * step)
        worked = jnp.dot(hidden, w_out[0, 0][:, columns], preferred_element_type=jnp.float32).astype(jnp.bfloat16)
        back = exchange(worked.reshape(experts, capacity, step)).reshape(rows, step)
        y = (h_rows[:, columns] + jnp.dot(mix, back, preferred_element_type=jnp.float32)).astype(jnp.bfloat16)
        across = lax.ppermute(y, "section", mirror)
        mirrored.append(across)
        if onward:
            handed.append(jnp.where(shared, across, lax.ppermute(y, "section", onward)))
        else:
            handed.append(across)
    return (jnp.concatenate(handed, axis=1)[None], jnp.concatenate(mirrored, axis=1)[None])


def solution(mesh):
    placed = (
        P("section", "expert", None),
        P("section", "expert", None),
        P("section", None, None),
        P("section", None),
        P("section", "expert", None),
        P("section", "expert", None, None),
        P("section", "expert", None, None),
    )
    return jax.shard_map(
        local,
        mesh=mesh,
        in_specs=placed,
        out_specs=(P("section", "expert", None), P("section", "expert", None)),
        check_vma=False,
    )
```

```python
import jax
import jax.numpy as jnp
from jax import lax
from jax.experimental import pallas as pl
from jax.experimental.pallas import tpu as pltpu
from jax.sharding import PartitionSpec as P

OUT_CHUNKS = 4
IN_CHUNKS = 2
VMEM = pl.BlockSpec(memory_space=pltpu.VMEM)
SMEM = pl.BlockSpec(memory_space=pltpu.SMEM)
HBM = pl.BlockSpec(memory_space=pl.ANY)
BF16 = jnp.bfloat16
F32 = jnp.float32


def inverse_rms(values):
    return lax.rsqrt(jnp.mean(values * values, axis=-1, keepdims=True) + 1e-06)


def matmul(a, b):
    return jnp.dot(a, b, preferred_element_type=F32)


def slot_table(me, ids, experts, slots):
    tokens = ids.shape[1]
    rows = experts * slots
    expert = lax.broadcasted_iota(jnp.int32, (experts, tokens), 0) ^ me
    named = jnp.zeros((experts, tokens), F32)
    for k in range(ids.shape[0]):
        named = named + jnp.where(ids[k : k + 1, :] == expert, 1.0, 0.0)
    before = lax.broadcasted_iota(jnp.int32, (tokens, tokens), 0)
    after = lax.broadcasted_iota(jnp.int32, (tokens, tokens), 1)
    earlier = jnp.where(before < after, 1.0, 0.0)
    tally = matmul(named.astype(BF16), earlier.astype(BF16))
    slot = jnp.where(named > 0.0, tally, -1.0)
    row = lax.broadcasted_iota(jnp.int32, (rows, experts), 0)
    low = lax.broadcasted_iota(jnp.int32, (rows, experts), 1) * slots
    spread = jnp.where((row >= low) & (row < low + slots), 1.0, 0.0)
    wanted = matmul(spread.astype(BF16), slot.astype(BF16))
    first = jnp.sum(spread * low.astype(F32), axis=1, keepdims=True)
    place = lax.broadcasted_iota(jnp.int32, (rows, 1), 0).astype(F32) - first
    return wanted == place, spread.astype(BF16), named, expert


def sum_rows(late, acts, skip, gain):
    skip = skip.astype(F32)
    term = gain * (skip * inverse_rms(skip))
    return acts.astype(F32) + jnp.where(late > 0, term, jnp.zeros_like(term))


def dispatch_kernel(experts, slots, pieces, late_ref, me_ref, ids_ref, gain_ref, acts_hbm, skip_hbm, *rest):
    out_refs, (acts_ref, skip_ref, normed_ref, sems) = rest[:-4], rest[-4:]
    tokens, width = acts_ref.shape
    size = tokens // pieces
    copies = []
    for r in range(pieces):
        part = pl.ds(r * size, size)
        pair = (
            pltpu.make_async_copy(skip_hbm.at[part], skip_ref.at[part], sems.at[0, r]),
            pltpu.make_async_copy(acts_hbm.at[part], acts_ref.at[part], sems.at[1, r]),
        )
        for copy in pair:
            copy.start()
        copies.append(pair)
    taken, _, _, _ = slot_table(me_ref[0], ids_ref[...], experts, slots)
    pick = jnp.where(taken, 1.0, 0.0).astype(BF16)
    for r in range(pieces):
        part = pl.ds(r * size, size)
        for copy in copies[r]:
            copy.wait()
        h = sum_rows(late_ref[0], acts_ref[part], skip_ref[part], gain_ref[...])
        normed_ref[part] = (h * inverse_rms(h)).astype(BF16)
    chips = experts // 2
    step = width // IN_CHUNKS
    for c in range(IN_CHUNKS):
        block = matmul(pick, normed_ref[:, c * step : (c + 1) * step]).astype(BF16)
        for k in range(chips):
            out_refs[c * chips + k][...] = block[k * 2 * slots : (k + 1) * 2 * slots]


def gate_kernel(experts, slots, late_ref, me_ref, ids_ref, gain_ref, acts_ref, skip_ref, router_ref, mix_ref, h_ref):
    h = sum_rows(late_ref[0], acts_ref[...], skip_ref[...], gain_ref[...])
    h_ref[...] = h
    normed = (h * inverse_rms(h)).astype(BF16)
    logits = lax.dot_general(
        router_ref[...], normed, (((1,), (1,)), ((), ())), preferred_element_type=F32
    )
    taken, spread, named, expert = slot_table(me_ref[0], ids_ref[...], experts, slots)
    natural = lax.broadcasted_iota(jnp.int32, (experts, ids_ref.shape[1]), 0)
    chosen = jnp.zeros(natural.shape, F32)
    for k in range(ids_ref.shape[0]):
        chosen = chosen + jnp.where(ids_ref[k : k + 1, :] == natural, 1.0, 0.0)
    peak = jnp.max(jnp.where(chosen > 0.0, logits, -jnp.inf), axis=0, keepdims=True)
    mass = jnp.where(chosen > 0.0, jnp.exp(logits - peak), 0.0)
    gates = (mass / jnp.sum(mass, axis=0, keepdims=True)).astype(BF16)
    order = lax.broadcasted_iota(jnp.int32, (experts, experts), 0) ^ me_ref[0]
    swap = jnp.where(order == lax.broadcasted_iota(jnp.int32, (experts, experts), 1), 1.0, 0.0)
    turned = matmul(swap.astype(BF16), gates).astype(BF16)
    wide = matmul(spread, turned)
    mix_ref[...] = jnp.where(taken, wide, 0.0).T.astype(BF16)


def first_kernel(chips, slots, last, *refs):
    blocks, (own_ref, other_ref) = refs[:chips], refs[chips : chips + 2]
    before_ref = None if len(refs) == chips + 4 else refs[chips + 2]
    out_ref, held = refs[-2:]

    @pl.when(pl.program_id(0) == 0)
    def _():
        for k in range(chips):
            for half in range(2):
                held[half, k * slots : (k + 1) * slots] = blocks[k][half * slots : (half + 1) * slots]

    size = chips * slots
    for half, weight in enumerate((own_ref, other_ref)):
        part = slice(half * size, (half + 1) * size)
        total = matmul(held[half], weight[...])
        if before_ref is not None:
            total = total + before_ref[part]
        out_ref[part] = jax.nn.gelu(total, approximate=True).astype(BF16) if last else total


def second_kernel(chips, slots, hidden_ref, own_ref, other_ref, *out_refs):
    size = chips * slots
    for half, weight in enumerate((own_ref, other_ref)):
        worked = matmul(hidden_ref[half * size : (half + 1) * size], weight[...]).astype(BF16)
        for k in range(chips):
            out_refs[k][half * slots : (half + 1) * slots] = worked[k * slots : (k + 1) * slots]


def combine_kernel(chips, h_ref, mix_ref, *refs):
    blocks, out_ref, held = refs[:chips], refs[-2], refs[-1]
    size = blocks[0].shape[0]
    for k in range(chips):
        held[k * size : (k + 1) * size] = blocks[k][...]
    out_ref[...] = (h_ref[...] + matmul(mix_ref[...], held[...])).astype(BF16)


def local(acts, expert_ids, router, skip_gain, skip_rows, w_in, w_out):
    section_pos = lax.axis_index("section")
    sections = lax.axis_size("section")
    devices = lax.axis_size("expert")
    tokens, width = acts.shape[1:]
    topk = expert_ids.shape[2]
    experts = router.shape[2]
    hidden_width = w_in.shape[3]
    capacity = 3 * tokens * topk // (2 * experts)
    slots = -(-capacity // 16) * 16
    rows = experts * slots
    chips = devices // 2
    params = pltpu.CompilerParams(vmem_limit_bytes=40 * 2**20)
    late = (section_pos >= sections // 2).astype(jnp.int32).reshape(1)
    me = lax.axis_index("expert").astype(jnp.int32).reshape(1)
    ids = expert_ids[0].T
    first, second = w_in[0, 0], w_out[0, 0]

    def across_core(block):
        return lax.ppermute(block, "expert", [(i, i ^ 1) for i in range(devices)])

    def exchange(blocks):
        return [blocks[0]] + [
            lax.ppermute(blocks[k], "expert", [(i, i ^ (2 * k)) for i in range(devices)])
            for k in range(1, chips)
        ]

    step = width // IN_CHUNKS
    pieces = 4
    sent = pl.pallas_call(
        lambda *refs: dispatch_kernel(experts, slots, pieces, *refs),
        out_shape=[jax.ShapeDtypeStruct((2 * slots, step), BF16)] * (chips * IN_CHUNKS),
        in_specs=[SMEM, SMEM, VMEM, VMEM, HBM, HBM],
        out_specs=[VMEM] * (chips * IN_CHUNKS),
        scratch_shapes=[
            pltpu.VMEM((tokens, width), BF16),
            pltpu.VMEM((tokens, width), BF16),
            pltpu.VMEM((tokens, width), BF16),
            pltpu.SemaphoreType.DMA((2, pieces)),
        ],
        compiler_params=params,
        name="dispatch",
    )(late, me, ids, skip_gain, acts[0], skip_rows[0])
    other_first = across_core(first)
    other_second = across_core(second)

    mix, h_rows = pl.pallas_call(
        lambda *refs: gate_kernel(experts, slots, *refs),
        out_shape=(
            jax.ShapeDtypeStruct((tokens, rows), BF16),
            jax.ShapeDtypeStruct((tokens, width), F32),
        ),
        in_specs=[SMEM, SMEM] + [VMEM] * 5,
        out_specs=(VMEM, VMEM),
        compiler_params=params,
        name="gates",
    )(late, me, ids, skip_gain, acts[0], skip_rows[0], router[0].T)

    steps = 4
    wide = hidden_width // steps
    total = None
    for c in range(IN_CHUNKS):
        arrived = exchange(sent[c * chips : (c + 1) * chips])
        last = c == IN_CHUNKS - 1
        weight = pl.BlockSpec((step, wide), lambda j, c=c: (c, j))
        column = pl.BlockSpec((rows, wide), lambda j: (0, j))
        total = pl.pallas_call(
            lambda *refs, last=last: first_kernel(chips, slots, last, *refs),
            grid=(steps,),
            out_shape=jax.ShapeDtypeStruct((rows, hidden_width), BF16 if last else F32),
            in_specs=[pl.BlockSpec((2 * slots, step), lambda j: (0, 0))] * chips
            + [weight, weight]
            + ([] if total is None else [column]),
            out_specs=column,
            scratch_shapes=[pltpu.VMEM((2, chips * slots, step), BF16)],
            compiler_params=params,
            name="first_matmul",
        )(*arrived, first, other_first, *([] if total is None else [total]))
    hidden = total

    mirror = [(s, sections - 1 - s) for s in range(sections)]
    same = [s for s in range(sections) if (s - 1) % sections == sections - 1 - s]
    onward = [((s - 1) % sections, s) for s in range(sections) if s not in same]
    shared = jnp.zeros((), jnp.bool_)
    for s in same:
        shared = shared | (section_pos == s)
    step = width // OUT_CHUNKS
    mirrored, handed = [], []
    for c in range(OUT_CHUNKS):
        weight = pl.BlockSpec((hidden_width, step), lambda j, c=c: (0, c))
        worked = pl.pallas_call(
            lambda *refs: second_kernel(chips, slots, *refs),
            grid=(1,),
            out_shape=[jax.ShapeDtypeStruct((2 * slots, step), BF16)] * chips,
            in_specs=[pl.BlockSpec((rows, hidden_width), lambda j: (0, 0)), weight, weight],
            out_specs=[pl.BlockSpec((2 * slots, step), lambda j: (0, 0))] * chips,
            compiler_params=params,
            name="second_matmul",
        )(hidden, second, other_second)
        back = exchange(worked)
        y = pl.pallas_call(
            lambda *refs: combine_kernel(chips, *refs),
            grid=(1,),
            out_shape=jax.ShapeDtypeStruct((tokens, step), BF16),
            in_specs=[
                pl.BlockSpec((tokens, step), lambda j, c=c: (0, c)),
                pl.BlockSpec((tokens, rows), lambda j: (0, 0)),
            ]
            + [pl.BlockSpec((2 * slots, step), lambda j: (0, 0))] * chips,
            out_specs=pl.BlockSpec((tokens, step), lambda j: (0, 0)),
            scratch_shapes=[pltpu.VMEM((rows, step), BF16)],
            compiler_params=params,
            name="combine",
        )(h_rows, mix, *back)
        across = lax.ppermute(y, "section", mirror)
        mirrored.append(across)
        handed.append(jnp.where(shared, across, lax.ppermute(y, "section", onward)) if onward else across)
    return (jnp.concatenate(handed, axis=1)[None], jnp.concatenate(mirrored, axis=1)[None])


def solution(mesh):
    placed = (
        P("section", "expert", None),
        P("section", "expert", None),
        P("section", None, None),
        P("section", None),
        P("section", "expert", None),
        P("section", "expert", None, None),
        P("section", "expert", None, None),
    )
    return jax.shard_map(
        local,
        mesh=mesh,
        in_specs=placed,
        out_specs=(P("section", "expert", None), P("section", "expert", None)),
        check_vma=False,
    )
```

```python
import jax
import jax.numpy as jnp
from jax import lax
from jax.experimental import pallas as pl
from jax.experimental.pallas import tpu as pltpu
from jax.sharding import PartitionSpec as P

VMEM = pl.BlockSpec(memory_space=pltpu.VMEM)
SMEM = pl.BlockSpec(memory_space=pltpu.SMEM)
HBM = pl.BlockSpec(memory_space=pltpu.HBM)
ANY = pl.BlockSpec(memory_space=pl.ANY)
BF16 = jnp.bfloat16
F32 = jnp.float32
IN_PARTS = (10, 6)
OUT_PARTS = (4, 5, 4, 3)


def cut(width, parts):
    unit, start, ranges = width // sum(parts), 0, []
    for part in parts:
        ranges.append((start, start + part * unit))
        start += part * unit
    return ranges


def inverse_rms(values):
    return lax.rsqrt(jnp.mean(values * values, axis=-1, keepdims=True) + 1e-06)


def matmul(a, b):
    return jnp.dot(a, b, preferred_element_type=F32)


def slot_table(me, ids, experts, slots):
    tokens = ids.shape[1]
    rows = experts * slots
    expert = lax.broadcasted_iota(jnp.int32, (experts, tokens), 0) ^ me
    named = jnp.zeros((experts, tokens), F32)
    for k in range(ids.shape[0]):
        named = named + jnp.where(ids[k : k + 1, :] == expert, 1.0, 0.0)
    before = lax.broadcasted_iota(jnp.int32, (tokens, tokens), 0)
    after = lax.broadcasted_iota(jnp.int32, (tokens, tokens), 1)
    earlier = jnp.where(before < after, 1.0, 0.0)
    tally = matmul(named.astype(BF16), earlier.astype(BF16))
    slot = jnp.where(named > 0.0, tally, -1.0)
    row = lax.broadcasted_iota(jnp.int32, (rows, experts), 0)
    low = lax.broadcasted_iota(jnp.int32, (rows, experts), 1) * slots
    spread = jnp.where((row >= low) & (row < low + slots), 1.0, 0.0)
    wanted = matmul(spread.astype(BF16), slot.astype(BF16))
    first = jnp.sum(spread * low.astype(F32), axis=1, keepdims=True)
    place = lax.broadcasted_iota(jnp.int32, (rows, 1), 0).astype(F32) - first
    return wanted == place, spread.astype(BF16), named, expert


def sum_rows(late, acts, skip, gain):
    skip = skip.astype(F32)
    term = gain * (skip * inverse_rms(skip))
    return acts.astype(F32) + jnp.where(late > 0, term, jnp.zeros_like(term))


def dispatch_kernel(experts, slots, pieces, columns, late_ref, me_ref, ids_hbm, gain_hbm, acts_hbm, skip_hbm, *rest):
    chips = experts // 2
    out_refs = rest[: chips * len(columns)]
    ids_ref, gain_ref, acts_ref, skip_ref, normed_ref, *held, sems, small, done = rest[chips * len(columns) :]
    tokens = acts_ref.shape[0]
    size = tokens // pieces
    ids_copy = pltpu.make_async_copy(ids_hbm, ids_ref, small.at[0])
    gain_copy = pltpu.make_async_copy(gain_hbm, gain_ref, small.at[1])
    ids_copy.start()
    gain_copy.start()
    copies = []
    for r in range(pieces):
        part = pl.ds(r * size, size)
        pair = (
            pltpu.make_async_copy(skip_hbm.at[part], skip_ref.at[part], sems.at[0, r]),
            pltpu.make_async_copy(acts_hbm.at[part], acts_ref.at[part], sems.at[1, r]),
        )
        for copy in pair:
            copy.start()
        copies.append(pair)
    ids_copy.wait()
    taken, _, _, _ = slot_table(me_ref[0], ids_ref[...], experts, slots)
    pick = jnp.where(taken, 1.0, 0.0).astype(BF16)
    gain_copy.wait()
    for r in range(pieces):
        part = pl.ds(r * size, size)
        for copy in copies[r]:
            copy.wait()
        h = sum_rows(late_ref[0], acts_ref[part], skip_ref[part], gain_ref[...])
        normed_ref[part] = (h * inverse_rms(h)).astype(BF16)
    sends = []
    for c, ends in enumerate(columns):
        held[c][...] = matmul(pick, normed_ref[:, ends[0] : ends[1]]).astype(BF16)
        for k in range(chips):
            block = held[c].at[pl.ds(k * 2 * slots, 2 * slots)]
            send = pltpu.make_async_copy(block, out_refs[c * chips + k], done.at[c * chips + k])
            send.start()
            sends.append(send)
    for send in sends:
        send.wait()


def gate_kernel(experts, slots, late_ref, me_ref, ids_ref, gain_ref, acts_ref, skip_ref, router_ref, mix_ref, h_ref):
    h = sum_rows(late_ref[0], acts_ref[...], skip_ref[...], gain_ref[...])
    h_ref[...] = h
    normed = (h * inverse_rms(h)).astype(BF16)
    logits = lax.dot_general(
        router_ref[...], normed, (((1,), (1,)), ((), ())), preferred_element_type=F32
    )
    taken, spread, named, expert = slot_table(me_ref[0], ids_ref[...], experts, slots)
    natural = lax.broadcasted_iota(jnp.int32, (experts, ids_ref.shape[1]), 0)
    chosen = jnp.zeros(natural.shape, F32)
    for k in range(ids_ref.shape[0]):
        chosen = chosen + jnp.where(ids_ref[k : k + 1, :] == natural, 1.0, 0.0)
    peak = jnp.max(jnp.where(chosen > 0.0, logits, -jnp.inf), axis=0, keepdims=True)
    mass = jnp.where(chosen > 0.0, jnp.exp(logits - peak), 0.0)
    gates = (mass / jnp.sum(mass, axis=0, keepdims=True)).astype(BF16)
    order = lax.broadcasted_iota(jnp.int32, (experts, experts), 0) ^ me_ref[0]
    swap = jnp.where(order == lax.broadcasted_iota(jnp.int32, (experts, experts), 1), 1.0, 0.0)
    turned = matmul(swap.astype(BF16), gates).astype(BF16)
    wide = matmul(spread, turned)
    mix_ref[...] = jnp.where(taken, wide, 0.0).T.astype(BF16)


def hold_kernel(source, target, sem):
    copy = pltpu.make_async_copy(source, target, sem)
    copy.start()
    copy.wait()


def first_kernel(chips, slots, columns, tile, first, last, *refs):
    blocks, (own_ref, other_ref, before_ref), (out_ref, held) = refs[:chips], refs[chips : chips + 3], refs[-2:]
    for k in range(chips):
        for half in range(2):
            held[half, k * slots : (k + 1) * slots] = blocks[k][half * slots : (half + 1) * slots]
    size = chips * slots
    for half, weight in enumerate((own_ref, other_ref)):
        part = slice(half * size, (half + 1) * size)
        for j in range(0, out_ref.shape[1], tile):
            total = matmul(held[half], weight[columns[0] : columns[1], j : j + tile])
            if not first:
                total = total + before_ref[part, j : j + tile]
            out_ref[part, j : j + tile] = jax.nn.gelu(total, approximate=True).astype(BF16) if last else total


def second_kernel(chips, slots, columns, hidden_ref, own_ref, other_ref, *refs):
    size = chips * slots
    out_refs = refs[-chips:]
    for half, weight in enumerate((own_ref, other_ref)):
        worked = matmul(hidden_ref[half * size : (half + 1) * size], weight[:, columns[0] : columns[1]]).astype(BF16)
        for k in range(chips):
            out_refs[k][half * slots : (half + 1) * slots] = worked[k * slots : (k + 1) * slots]


def combine_kernel(chips, columns, h_ref, mix_ref, *refs):
    blocks, out_ref, held = refs[:chips], refs[-2], refs[-1]
    size = blocks[0].shape[0]
    for k in range(chips):
        held[k * size : (k + 1) * size] = blocks[k][...]
    out_ref[...] = (h_ref[:, columns[0] : columns[1]] + matmul(mix_ref[...], held[...])).astype(BF16)


def place_kernel(columns, shared_ref, across_ref, onward_ref, *refs):
    handed_ref, mirrored_ref, sems = refs[-3:]
    part = pl.ds(columns[0], columns[1] - columns[0])
    copy = pltpu.make_async_copy(across_ref, mirrored_ref.at[:, part], sems.at[0])
    copy.start()

    @pl.when(shared_ref[0] > 0)
    def _():
        again = pltpu.make_async_copy(across_ref, handed_ref.at[:, part], sems.at[1])
        again.start()
        again.wait()

    @pl.when(shared_ref[0] == 0)
    def _():
        again = pltpu.make_async_copy(onward_ref, handed_ref.at[:, part], sems.at[1])
        again.start()
        again.wait()

    copy.wait()


def local(acts, expert_ids, router, skip_gain, skip_rows, w_in, w_out):
    section_pos = lax.axis_index("section")
    sections = lax.axis_size("section")
    devices = lax.axis_size("expert")
    tokens, width = acts.shape[1:]
    topk = expert_ids.shape[2]
    experts = router.shape[2]
    hidden_width = w_in.shape[3]
    capacity = 3 * tokens * topk // (2 * experts)
    slots = -(-capacity // 16) * 16
    rows = experts * slots
    chips = devices // 2

    def params(mib):
        return pltpu.CompilerParams(vmem_limit_bytes=mib * 2**20)

    late = (section_pos >= sections // 2).astype(jnp.int32).reshape(1)
    me = lax.axis_index("expert").astype(jnp.int32).reshape(1)
    ids = expert_ids[0].T
    first, second = w_in[0, 0], w_out[0, 0]

    def across_core(block):
        return lax.ppermute(block, "expert", [(i, i ^ 1) for i in range(devices)])

    def exchange(blocks):
        return [blocks[0]] + [
            lax.ppermute(blocks[k], "expert", [(i, i ^ (2 * k)) for i in range(devices)])
            for k in range(1, chips)
        ]

    incoming = cut(width, IN_PARTS)
    outgoing = cut(width, OUT_PARTS)

    def sendable(ends):
        return [jax.ShapeDtypeStruct((2 * slots, ends[1] - ends[0]), BF16)] * chips

    pieces = 4
    sent = pl.pallas_call(
        lambda *refs: dispatch_kernel(experts, slots, pieces, incoming, *refs),
        out_shape=[shape for ends in incoming for shape in sendable(ends)],
        in_specs=[SMEM, SMEM, HBM, HBM, HBM, HBM],
        out_specs=[HBM] * (chips * len(incoming)),
        scratch_shapes=[
            pltpu.VMEM((topk, tokens), jnp.int32),
            pltpu.VMEM((1, width), F32),
            pltpu.VMEM((tokens, width), BF16),
            pltpu.VMEM((tokens, width), BF16),
            pltpu.VMEM((tokens, width), BF16),
        ]
        + [pltpu.VMEM((rows, ends[1] - ends[0]), BF16) for ends in incoming]
        + [
            pltpu.SemaphoreType.DMA((2, pieces)),
            pltpu.SemaphoreType.DMA((2,)),
            pltpu.SemaphoreType.DMA((chips * len(incoming),)),
        ],
        compiler_params=params(62),
        name="dispatch",
    )(late, me, ids, skip_gain, acts[0], skip_rows[0])

    def hold(block):
        return pl.pallas_call(
            hold_kernel,
            out_shape=jax.ShapeDtypeStruct(block.shape, block.dtype),
            in_specs=[ANY],
            out_specs=VMEM,
            scratch_shapes=[pltpu.SemaphoreType.DMA],
            compiler_params=params(16),
            name="hold",
        )(block)

    other_first = hold(across_core(first))
    other_second = hold(across_core(second))

    mix, h_rows = pl.pallas_call(
        lambda *refs: gate_kernel(experts, slots, *refs),
        out_shape=(
            jax.ShapeDtypeStruct((tokens, rows), BF16),
            jax.ShapeDtypeStruct((tokens, width), F32),
        ),
        in_specs=[SMEM, SMEM] + [VMEM] * 5,
        out_specs=(VMEM, VMEM),
        compiler_params=params(16),
        name="gates",
    )(late, me, ids, skip_gain, acts[0], skip_rows[0], router[0].T)

    total = mix
    for c, ends in enumerate(incoming):
        arrived = exchange(sent[c * chips : (c + 1) * chips])
        last = c == len(incoming) - 1
        total = pl.pallas_call(
            lambda *refs, c=c, ends=ends, last=last: first_kernel(
                chips, slots, ends, min(512, hidden_width), c == 0, last, *refs
            ),
            out_shape=jax.ShapeDtypeStruct((rows, hidden_width), BF16 if last else F32),
            in_specs=[VMEM] * (chips + 2) + [ANY if c == 0 else VMEM, ANY],
            out_specs=VMEM,
            scratch_shapes=[pltpu.VMEM((2, chips * slots, ends[1] - ends[0]), BF16)],
            compiler_params=params(16),
            name="first_matmul",
        )(*arrived, first, other_first, total, mix if c == 0 else other_second)
    hidden = total

    mirror = [(s, sections - 1 - s) for s in range(sections)]
    same = [s for s in range(sections) if (s - 1) % sections == sections - 1 - s]
    onward = [((s - 1) % sections, s) for s in range(sections) if s not in same]
    shared = jnp.zeros((), jnp.bool_)
    for s in same:
        shared = shared | (section_pos == s)
    shared = shared.astype(jnp.int32).reshape(1)
    made, gone, placed = [], [], []
    for c, ends in enumerate(outgoing):
        after = gone[c - 2] + [made[c - 1]] if c >= 2 else []
        worked = pl.pallas_call(
            lambda *refs, ends=ends: second_kernel(chips, slots, ends, *refs),
            out_shape=sendable(ends),
            in_specs=[VMEM] * 3 + [ANY] * len(after),
            out_specs=[VMEM] * chips,
            compiler_params=params(16),
            name="second_matmul",
        )(hidden, second, other_second, *after)
        back = exchange(worked)
        later = gone[c - 1] if c == len(outgoing) - 1 else []
        y = pl.pallas_call(
            lambda *refs, ends=ends: combine_kernel(chips, ends, *refs),
            out_shape=jax.ShapeDtypeStruct((tokens, ends[1] - ends[0]), BF16),
            in_specs=[VMEM] * (chips + 2) + [ANY] * len(later),
            out_specs=VMEM,
            scratch_shapes=[pltpu.VMEM((rows, ends[1] - ends[0]), BF16)],
            compiler_params=params(16),
            name="combine",
        )(h_rows, mix, *back, *later)
        made.append(y)
        across = lax.ppermute(y, "section", mirror)
        ahead = lax.ppermute(y, "section", onward) if onward else across
        gone.append([across, ahead])
        placed = pl.pallas_call(
            lambda *refs, ends=ends: place_kernel(ends, *refs),
            out_shape=[jax.ShapeDtypeStruct((tokens, width), BF16)] * 2,
            in_specs=[SMEM, ANY, ANY] + [HBM] * len(placed),
            out_specs=[HBM, HBM],
            scratch_shapes=[pltpu.SemaphoreType.DMA((2,))],
            input_output_aliases={3: 0, 4: 1} if placed else {},
            compiler_params=params(16),
            name="place",
        )(shared, across, ahead, *placed)
    return (placed[0][None], placed[1][None])


def solution(mesh):
    placed = (
        P("section", "expert", None),
        P("section", "expert", None),
        P("section", None, None),
        P("section", None),
        P("section", "expert", None),
        P("section", "expert", None, None),
        P("section", "expert", None, None),
    )
    return jax.shard_map(
        local,
        mesh=mesh,
        in_specs=placed,
        out_specs=(P("section", "expert", None), P("section", "expert", None)),
        check_vma=False,
    )
```

```python
import jax
import jax.numpy as jnp
from jax import lax
from jax.experimental import pallas as pl
from jax.experimental.pallas import tpu as pltpu
from jax.sharding import PartitionSpec as P

VMEM = pl.BlockSpec(memory_space=pltpu.VMEM)
SMEM = pl.BlockSpec(memory_space=pltpu.SMEM)
HBM = pl.BlockSpec(memory_space=pltpu.HBM)
ANY = pl.BlockSpec(memory_space=pl.ANY)
BF16 = jnp.bfloat16
F32 = jnp.float32
IN_PARTS = (5, 7, 4)
OUT_PARTS = (4, 5, 4, 3)


def cut(width, parts):
    unit, start, ranges = width // sum(parts), 0, []
    for part in parts:
        ranges.append((start, start + part * unit))
        start += part * unit
    return ranges


def inverse_rms(values):
    return lax.rsqrt(jnp.mean(values * values, axis=-1, keepdims=True) + 1e-06)


def matmul(a, b):
    return jnp.dot(a, b, preferred_element_type=F32)


def slot_table(me, ids, experts, slots):
    tokens = ids.shape[1]
    rows = experts * slots
    expert = lax.broadcasted_iota(jnp.int32, (experts, tokens), 0) ^ me
    named = jnp.zeros((experts, tokens), F32)
    for k in range(ids.shape[0]):
        named = named + jnp.where(ids[k : k + 1, :] == expert, 1.0, 0.0)
    before = lax.broadcasted_iota(jnp.int32, (tokens, tokens), 0)
    after = lax.broadcasted_iota(jnp.int32, (tokens, tokens), 1)
    earlier = jnp.where(before < after, 1.0, 0.0)
    tally = matmul(named.astype(BF16), earlier.astype(BF16))
    slot = jnp.where(named > 0.0, tally, -1.0)
    row = lax.broadcasted_iota(jnp.int32, (rows, experts), 0)
    low = lax.broadcasted_iota(jnp.int32, (rows, experts), 1) * slots
    spread = jnp.where((row >= low) & (row < low + slots), 1.0, 0.0)
    wanted = matmul(spread.astype(BF16), slot.astype(BF16))
    first = jnp.sum(spread * low.astype(F32), axis=1, keepdims=True)
    place = lax.broadcasted_iota(jnp.int32, (rows, 1), 0).astype(F32) - first
    return wanted == place, spread.astype(BF16), named, expert


def sum_rows(late, acts, skip, gain):
    skip = skip.astype(F32)
    term = gain * (skip * inverse_rms(skip))
    return acts.astype(F32) + jnp.where(late > 0, term, jnp.zeros_like(term))


def dispatch_kernel(experts, slots, pieces, columns, late_ref, me_ref, ids_hbm, gain_hbm, acts_hbm, skip_hbm, *rest):
    chips = experts // 2
    out_refs = rest[: chips * len(columns)]
    ids_ref, gain_ref, acts_ref, skip_ref, normed_ref, *held, sems, small, done = rest[chips * len(columns) :]
    tokens = acts_ref.shape[0]
    size = tokens // pieces
    ids_copy = pltpu.make_async_copy(ids_hbm, ids_ref, small.at[0])
    gain_copy = pltpu.make_async_copy(gain_hbm, gain_ref, small.at[1])
    ids_copy.start()
    gain_copy.start()
    copies = []
    for r in range(pieces):
        part = pl.ds(r * size, size)
        pair = (
            pltpu.make_async_copy(skip_hbm.at[part], skip_ref.at[part], sems.at[0, r]),
            pltpu.make_async_copy(acts_hbm.at[part], acts_ref.at[part], sems.at[1, r]),
        )
        for copy in pair:
            copy.start()
        copies.append(pair)
    ids_copy.wait()
    taken, _, _, _ = slot_table(me_ref[0], ids_ref[...], experts, slots)
    pick = jnp.where(taken, 1.0, 0.0).astype(BF16)
    gain_copy.wait()
    for r in range(pieces):
        part = pl.ds(r * size, size)
        for copy in copies[r]:
            copy.wait()
        h = sum_rows(late_ref[0], acts_ref[part], skip_ref[part], gain_ref[...])
        normed_ref[part] = (h * inverse_rms(h)).astype(BF16)
    sends = []
    for c, ends in enumerate(columns):
        held[c][...] = matmul(pick, normed_ref[:, ends[0] : ends[1]]).astype(BF16)
        for k in range(chips):
            block = held[c].at[pl.ds(k * 2 * slots, 2 * slots)]
            send = pltpu.make_async_copy(block, out_refs[c * chips + k], done.at[c * chips + k])
            send.start()
            sends.append(send)
    for send in sends:
        send.wait()


def gate_kernel(experts, slots, late_ref, me_ref, ids_ref, gain_ref, acts_ref, skip_ref, router_ref, mix_ref, h_ref):
    h = sum_rows(late_ref[0], acts_ref[...], skip_ref[...], gain_ref[...])
    h_ref[...] = h
    normed = (h * inverse_rms(h)).astype(BF16)
    logits = lax.dot_general(
        router_ref[...], normed, (((1,), (1,)), ((), ())), preferred_element_type=F32
    )
    taken, spread, named, expert = slot_table(me_ref[0], ids_ref[...], experts, slots)
    natural = lax.broadcasted_iota(jnp.int32, (experts, ids_ref.shape[1]), 0)
    chosen = jnp.zeros(natural.shape, F32)
    for k in range(ids_ref.shape[0]):
        chosen = chosen + jnp.where(ids_ref[k : k + 1, :] == natural, 1.0, 0.0)
    peak = jnp.max(jnp.where(chosen > 0.0, logits, -jnp.inf), axis=0, keepdims=True)
    mass = jnp.where(chosen > 0.0, jnp.exp(logits - peak), 0.0)
    gates = (mass / jnp.sum(mass, axis=0, keepdims=True)).astype(BF16)
    order = lax.broadcasted_iota(jnp.int32, (experts, experts), 0) ^ me_ref[0]
    swap = jnp.where(order == lax.broadcasted_iota(jnp.int32, (experts, experts), 1), 1.0, 0.0)
    turned = matmul(swap.astype(BF16), gates).astype(BF16)
    wide = matmul(spread, turned)
    mix_ref[...] = jnp.where(taken, wide, 0.0).T.astype(BF16)


def hold_kernel(source, target, sem):
    copy = pltpu.make_async_copy(source, target, sem)
    copy.start()
    copy.wait()


def first_kernel(chips, slots, columns, tile, first, last, *refs):
    blocks, (own_ref, other_ref, before_ref), (out_ref, held) = refs[:chips], refs[chips : chips + 3], refs[-2:]
    for k in range(chips):
        for half in range(2):
            held[half, k * slots : (k + 1) * slots] = blocks[k][half * slots : (half + 1) * slots]
    size = chips * slots
    for half, weight in enumerate((own_ref, other_ref)):
        part = slice(half * size, (half + 1) * size)
        for j in range(0, out_ref.shape[1], tile):
            total = matmul(held[half], weight[columns[0] : columns[1], j : j + tile])
            if not first:
                total = total + before_ref[part, j : j + tile]
            out_ref[part, j : j + tile] = jax.nn.gelu(total, approximate=True).astype(BF16) if last else total


def second_kernel(chips, slots, columns, hidden_ref, own_ref, other_ref, *refs):
    size = chips * slots
    out_refs = refs[-chips:]
    for half, weight in enumerate((own_ref, other_ref)):
        worked = matmul(hidden_ref[half * size : (half + 1) * size], weight[:, columns[0] : columns[1]]).astype(BF16)
        for k in range(chips):
            out_refs[k][half * slots : (half + 1) * slots] = worked[k * slots : (k + 1) * slots]


def combine_kernel(chips, columns, h_ref, mix_ref, *refs):
    blocks, out_ref, held = refs[:chips], refs[-2], refs[-1]
    size = blocks[0].shape[0]
    for k in range(chips):
        held[k * size : (k + 1) * size] = blocks[k][...]
    out_ref[...] = (h_ref[:, columns[0] : columns[1]] + matmul(mix_ref[...], held[...])).astype(BF16)


def place_kernel(columns, shared_ref, across_ref, onward_ref, *refs):
    handed_ref, mirrored_ref, sems = refs[-3:]
    part = pl.ds(columns[0], columns[1] - columns[0])
    copy = pltpu.make_async_copy(across_ref, mirrored_ref.at[:, part], sems.at[0])
    copy.start()

    @pl.when(shared_ref[0] > 0)
    def _():
        again = pltpu.make_async_copy(across_ref, handed_ref.at[:, part], sems.at[1])
        again.start()
        again.wait()

    @pl.when(shared_ref[0] == 0)
    def _():
        again = pltpu.make_async_copy(onward_ref, handed_ref.at[:, part], sems.at[1])
        again.start()
        again.wait()

    copy.wait()


def local(acts, expert_ids, router, skip_gain, skip_rows, w_in, w_out):
    section_pos = lax.axis_index("section")
    sections = lax.axis_size("section")
    devices = lax.axis_size("expert")
    tokens, width = acts.shape[1:]
    topk = expert_ids.shape[2]
    experts = router.shape[2]
    hidden_width = w_in.shape[3]
    capacity = 3 * tokens * topk // (2 * experts)
    slots = -(-capacity // 16) * 16
    rows = experts * slots
    chips = devices // 2

    def params(mib):
        return pltpu.CompilerParams(vmem_limit_bytes=mib * 2**20)

    late = (section_pos >= sections // 2).astype(jnp.int32).reshape(1)
    me = lax.axis_index("expert").astype(jnp.int32).reshape(1)
    ids = expert_ids[0].T
    first, second = w_in[0, 0], w_out[0, 0]

    def across_core(block):
        return lax.ppermute(block, "expert", [(i, i ^ 1) for i in range(devices)])

    def exchange(blocks):
        return [blocks[0]] + [
            lax.ppermute(blocks[k], "expert", [(i, i ^ (2 * k)) for i in range(devices)])
            for k in range(1, chips)
        ]

    incoming = cut(width, IN_PARTS)
    outgoing = cut(width, OUT_PARTS)

    def sendable(ends):
        return [jax.ShapeDtypeStruct((2 * slots, ends[1] - ends[0]), BF16)] * chips

    pieces = 2
    def dispatch(columns, mib):
        return pl.pallas_call(
            lambda *refs: dispatch_kernel(experts, slots, pieces, columns, *refs),
            out_shape=[shape for ends in columns for shape in sendable(ends)],
            in_specs=[SMEM, SMEM, HBM, HBM, HBM, HBM],
            out_specs=[HBM] * (chips * len(columns)),
            scratch_shapes=[
                pltpu.VMEM((topk, tokens), jnp.int32),
                pltpu.VMEM((1, width), F32),
                pltpu.VMEM((tokens, width), BF16),
                pltpu.VMEM((tokens, width), BF16),
                pltpu.VMEM((tokens, width), BF16),
            ]
            + [pltpu.VMEM((rows, ends[1] - ends[0]), BF16) for ends in columns]
            + [
                pltpu.SemaphoreType.DMA((2, pieces)),
                pltpu.SemaphoreType.DMA((2,)),
                pltpu.SemaphoreType.DMA((chips * len(columns),)),
            ],
            compiler_params=params(mib),
            name="dispatch",
        )(late, me, ids, skip_gain, acts[0], skip_rows[0])

    sent = [*dispatch(incoming[:1], 62), *dispatch(incoming[1:], 24)]

    def hold(block):
        return pl.pallas_call(
            hold_kernel,
            out_shape=jax.ShapeDtypeStruct(block.shape, block.dtype),
            in_specs=[ANY],
            out_specs=VMEM,
            scratch_shapes=[pltpu.SemaphoreType.DMA],
            compiler_params=params(16),
            name="hold",
        )(block)

    other_first = hold(across_core(first))
    other_second = hold(across_core(second))

    mix, h_rows = pl.pallas_call(
        lambda *refs: gate_kernel(experts, slots, *refs),
        out_shape=(
            jax.ShapeDtypeStruct((tokens, rows), BF16),
            jax.ShapeDtypeStruct((tokens, width), F32),
        ),
        in_specs=[SMEM, SMEM] + [VMEM] * 5,
        out_specs=(VMEM, VMEM),
        compiler_params=params(16),
        name="gates",
    )(late, me, ids, skip_gain, acts[0], skip_rows[0], router[0].T)

    total = mix
    for c, ends in enumerate(incoming):
        arrived = exchange(sent[c * chips : (c + 1) * chips])
        last = c == len(incoming) - 1
        total = pl.pallas_call(
            lambda *refs, c=c, ends=ends, last=last: first_kernel(
                chips, slots, ends, min(512, hidden_width), c == 0, last, *refs
            ),
            out_shape=jax.ShapeDtypeStruct((rows, hidden_width), BF16 if last else F32),
            in_specs=[VMEM] * (chips + 2) + [ANY if c == 0 else VMEM, ANY],
            out_specs=VMEM,
            scratch_shapes=[pltpu.VMEM((2, chips * slots, ends[1] - ends[0]), BF16)],
            compiler_params=params(16),
            name="first_matmul",
        )(*arrived, first, other_first, total, mix if c == 0 else other_second)
    hidden = total

    mirror = [(s, sections - 1 - s) for s in range(sections)]
    same = [s for s in range(sections) if (s - 1) % sections == sections - 1 - s]
    onward = [((s - 1) % sections, s) for s in range(sections) if s not in same]
    shared = jnp.zeros((), jnp.bool_)
    for s in same:
        shared = shared | (section_pos == s)
    shared = shared.astype(jnp.int32).reshape(1)
    made, gone, placed = [], [], []
    for c, ends in enumerate(outgoing):
        after = gone[c - 2] + [made[c - 1]] if c >= 2 else []
        worked = pl.pallas_call(
            lambda *refs, ends=ends: second_kernel(chips, slots, ends, *refs),
            out_shape=sendable(ends),
            in_specs=[VMEM] * 3 + [ANY] * len(after),
            out_specs=[VMEM] * chips,
            compiler_params=params(16),
            name="second_matmul",
        )(hidden, second, other_second, *after)
        back = exchange(worked)
        later = gone[c - 1] if c == len(outgoing) - 1 else []
        y = pl.pallas_call(
            lambda *refs, ends=ends: combine_kernel(chips, ends, *refs),
            out_shape=jax.ShapeDtypeStruct((tokens, ends[1] - ends[0]), BF16),
            in_specs=[VMEM] * (chips + 2) + [ANY] * len(later),
            out_specs=VMEM,
            scratch_shapes=[pltpu.VMEM((rows, ends[1] - ends[0]), BF16)],
            compiler_params=params(16),
            name="combine",
        )(h_rows, mix, *back, *later)
        made.append(y)
        across = lax.ppermute(y, "section", mirror)
        ahead = lax.ppermute(y, "section", onward) if onward else across
        gone.append([across, ahead])
        placed = pl.pallas_call(
            lambda *refs, ends=ends: place_kernel(ends, *refs),
            out_shape=[jax.ShapeDtypeStruct((tokens, width), BF16)] * 2,
            in_specs=[SMEM, ANY, ANY] + [HBM] * len(placed),
            out_specs=[HBM, HBM],
            scratch_shapes=[pltpu.SemaphoreType.DMA((2,))],
            input_output_aliases={3: 0, 4: 1} if placed else {},
            compiler_params=params(16),
            name="place",
        )(shared, across, ahead, *placed)
    return (placed[0][None], placed[1][None])


def solution(mesh):
    placed = (
        P("section", "expert", None),
        P("section", "expert", None),
        P("section", None, None),
        P("section", None),
        P("section", "expert", None),
        P("section", "expert", None, None),
        P("section", "expert", None, None),
    )
    return jax.shard_map(
        local,
        mesh=mesh,
        in_specs=placed,
        out_specs=(P("section", "expert", None), P("section", "expert", None)),
        check_vma=False,
    )
```

```python
import jax
import jax.numpy as jnp
from jax import lax
from jax.experimental import pallas as pl
from jax.experimental.pallas import tpu as pltpu
from jax.sharding import PartitionSpec as P

VMEM = pl.BlockSpec(memory_space=pltpu.VMEM)
SMEM = pl.BlockSpec(memory_space=pltpu.SMEM)
HBM = pl.BlockSpec(memory_space=pltpu.HBM)
ANY = pl.BlockSpec(memory_space=pl.ANY)
BF16 = jnp.bfloat16
F32 = jnp.float32
IN_PARTS = (5, 7, 4)
OUT_PARTS = (5, 7, 4)


def cut(width, parts):
    unit, start, ranges = width // sum(parts), 0, []
    for part in parts:
        ranges.append((start, start + part * unit))
        start += part * unit
    return ranges


def inverse_rms(values):
    return lax.rsqrt(jnp.mean(values * values, axis=-1, keepdims=True) + 1e-06)


def matmul(a, b):
    return jnp.dot(a, b, preferred_element_type=F32)


def slot_table(me, ids, experts, slots):
    tokens = ids.shape[1]
    rows = experts * slots
    expert = lax.broadcasted_iota(jnp.int32, (experts, tokens), 0) ^ me
    named = jnp.zeros((experts, tokens), F32)
    for k in range(ids.shape[0]):
        named = named + jnp.where(ids[k : k + 1, :] == expert, 1.0, 0.0)
    before = lax.broadcasted_iota(jnp.int32, (tokens, tokens), 0)
    after = lax.broadcasted_iota(jnp.int32, (tokens, tokens), 1)
    earlier = jnp.where(before < after, 1.0, 0.0)
    tally = matmul(named.astype(BF16), earlier.astype(BF16))
    slot = jnp.where(named > 0.0, tally, -1.0)
    row = lax.broadcasted_iota(jnp.int32, (rows, experts), 0)
    low = lax.broadcasted_iota(jnp.int32, (rows, experts), 1) * slots
    spread = jnp.where((row >= low) & (row < low + slots), 1.0, 0.0)
    wanted = matmul(spread.astype(BF16), slot.astype(BF16))
    first = jnp.sum(spread * low.astype(F32), axis=1, keepdims=True)
    place = lax.broadcasted_iota(jnp.int32, (rows, 1), 0).astype(F32) - first
    return wanted == place, spread.astype(BF16), named, expert


def sum_rows(late, acts, skip, gain):
    skip = skip.astype(F32)
    term = gain * (skip * inverse_rms(skip))
    return acts.astype(F32) + jnp.where(late > 0, term, jnp.zeros_like(term))


def dispatch_kernel(experts, slots, pieces, columns, late_ref, me_ref, ids_hbm, gain_hbm, acts_hbm, skip_hbm, *rest):
    chips = experts // 2
    out_refs = rest[: chips * len(columns)]
    ids_ref, gain_ref, acts_ref, skip_ref, normed_ref, *held, sems, small, done = rest[chips * len(columns) :]
    tokens = acts_ref.shape[0]
    size = tokens // pieces
    ids_copy = pltpu.make_async_copy(ids_hbm, ids_ref, small.at[0])
    gain_copy = pltpu.make_async_copy(gain_hbm, gain_ref, small.at[1])
    ids_copy.start()
    gain_copy.start()
    copies = []
    for r in range(pieces):
        part = pl.ds(r * size, size)
        pair = (
            pltpu.make_async_copy(skip_hbm.at[part], skip_ref.at[part], sems.at[0, r]),
            pltpu.make_async_copy(acts_hbm.at[part], acts_ref.at[part], sems.at[1, r]),
        )
        for copy in pair:
            copy.start()
        copies.append(pair)
    ids_copy.wait()
    taken, _, _, _ = slot_table(me_ref[0], ids_ref[...], experts, slots)
    pick = jnp.where(taken, 1.0, 0.0).astype(BF16)
    gain_copy.wait()
    for r in range(pieces):
        part = pl.ds(r * size, size)
        for copy in copies[r]:
            copy.wait()
        h = sum_rows(late_ref[0], acts_ref[part], skip_ref[part], gain_ref[...])
        normed_ref[part] = (h * inverse_rms(h)).astype(BF16)
    sends = []
    for c, ends in enumerate(columns):
        held[c][...] = matmul(pick, normed_ref[:, ends[0] : ends[1]]).astype(BF16)
        for k in range(chips):
            block = held[c].at[pl.ds(k * 2 * slots, 2 * slots)]
            send = pltpu.make_async_copy(block, out_refs[c * chips + k], done.at[c * chips + k])
            send.start()
            sends.append(send)
    for send in sends:
        send.wait()


def gate_kernel(experts, slots, late_ref, me_ref, ids_ref, gain_ref, acts_ref, skip_ref, router_ref, mix_ref, h_ref):
    h = sum_rows(late_ref[0], acts_ref[...], skip_ref[...], gain_ref[...])
    h_ref[...] = h
    normed = (h * inverse_rms(h)).astype(BF16)
    logits = lax.dot_general(
        router_ref[...], normed, (((1,), (1,)), ((), ())), preferred_element_type=F32
    )
    taken, spread, named, expert = slot_table(me_ref[0], ids_ref[...], experts, slots)
    natural = lax.broadcasted_iota(jnp.int32, (experts, ids_ref.shape[1]), 0)
    chosen = jnp.zeros(natural.shape, F32)
    for k in range(ids_ref.shape[0]):
        chosen = chosen + jnp.where(ids_ref[k : k + 1, :] == natural, 1.0, 0.0)
    peak = jnp.max(jnp.where(chosen > 0.0, logits, -jnp.inf), axis=0, keepdims=True)
    mass = jnp.where(chosen > 0.0, jnp.exp(logits - peak), 0.0)
    gates = (mass / jnp.sum(mass, axis=0, keepdims=True)).astype(BF16)
    order = lax.broadcasted_iota(jnp.int32, (experts, experts), 0) ^ me_ref[0]
    swap = jnp.where(order == lax.broadcasted_iota(jnp.int32, (experts, experts), 1), 1.0, 0.0)
    turned = matmul(swap.astype(BF16), gates).astype(BF16)
    wide = matmul(spread, turned)
    mix_ref[...] = jnp.where(taken, wide, 0.0).T.astype(BF16)


def hold_kernel(source, target, sem):
    copy = pltpu.make_async_copy(source, target, sem)
    copy.start()
    copy.wait()


def first_kernel(chips, slots, columns, tile, first, last, *refs):
    blocks, (own_ref, other_ref, before_ref), (out_ref, held) = refs[:chips], refs[chips : chips + 3], refs[-2:]
    for k in range(chips):
        for half in range(2):
            held[half, k * slots : (k + 1) * slots] = blocks[k][half * slots : (half + 1) * slots]
    size = chips * slots
    for half, weight in enumerate((own_ref, other_ref)):
        part = slice(half * size, (half + 1) * size)
        for j in range(0, out_ref.shape[1], tile):
            total = matmul(held[half], weight[columns[0] : columns[1], j : j + tile])
            if not first:
                total = total + before_ref[part, j : j + tile]
            out_ref[part, j : j + tile] = jax.nn.gelu(total, approximate=True).astype(BF16) if last else total


def second_kernel(chips, slots, columns, hidden_ref, own_ref, other_ref, *refs):
    size = chips * slots
    out_refs = refs[-chips:]
    for half, weight in enumerate((own_ref, other_ref)):
        worked = matmul(hidden_ref[half * size : (half + 1) * size], weight[:, columns[0] : columns[1]]).astype(BF16)
        for k in range(chips):
            out_refs[k][half * slots : (half + 1) * slots] = worked[k * slots : (k + 1) * slots]


def combine_kernel(chips, columns, h_ref, mix_ref, *refs):
    blocks, out_ref, held = refs[:chips], refs[-2], refs[-1]
    size = blocks[0].shape[0]
    for k in range(chips):
        held[k * size : (k + 1) * size] = blocks[k][...]
    out_ref[...] = (h_ref[:, columns[0] : columns[1]] + matmul(mix_ref[...], held[...])).astype(BF16)


def place_kernel(columns, shared_ref, across_ref, onward_ref, *refs):
    handed_ref, mirrored_ref, sems = refs[-3:]
    part = pl.ds(columns[0], columns[1] - columns[0])
    copy = pltpu.make_async_copy(across_ref, mirrored_ref.at[:, part], sems.at[0])
    copy.start()

    @pl.when(shared_ref[0] > 0)
    def _():
        again = pltpu.make_async_copy(across_ref, handed_ref.at[:, part], sems.at[1])
        again.start()
        again.wait()

    @pl.when(shared_ref[0] == 0)
    def _():
        again = pltpu.make_async_copy(onward_ref, handed_ref.at[:, part], sems.at[1])
        again.start()
        again.wait()

    copy.wait()


def local(acts, expert_ids, router, skip_gain, skip_rows, w_in, w_out):
    section_pos = lax.axis_index("section")
    sections = lax.axis_size("section")
    devices = lax.axis_size("expert")
    tokens, width = acts.shape[1:]
    topk = expert_ids.shape[2]
    experts = router.shape[2]
    hidden_width = w_in.shape[3]
    capacity = 3 * tokens * topk // (2 * experts)
    slots = -(-capacity // 16) * 16
    rows = experts * slots
    chips = devices // 2

    def params(mib):
        return pltpu.CompilerParams(vmem_limit_bytes=mib * 2**20)

    late = (section_pos >= sections // 2).astype(jnp.int32).reshape(1)
    me = lax.axis_index("expert").astype(jnp.int32).reshape(1)
    ids = expert_ids[0].T
    first, second = w_in[0, 0], w_out[0, 0]

    def across_core(block):
        return lax.ppermute(block, "expert", [(i, i ^ 1) for i in range(devices)])

    def exchange(blocks):
        return [blocks[0]] + [
            lax.ppermute(blocks[k], "expert", [(i, i ^ (2 * k)) for i in range(devices)])
            for k in range(1, chips)
        ]

    incoming = cut(width, IN_PARTS)
    outgoing = cut(width, OUT_PARTS)

    def sendable(ends):
        return [jax.ShapeDtypeStruct((2 * slots, ends[1] - ends[0]), BF16)] * chips

    pieces = 2
    def dispatch(columns, mib):
        return pl.pallas_call(
            lambda *refs: dispatch_kernel(experts, slots, pieces, columns, *refs),
            out_shape=[shape for ends in columns for shape in sendable(ends)],
            in_specs=[SMEM, SMEM, HBM, HBM, HBM, HBM],
            out_specs=[HBM] * (chips * len(columns)),
            scratch_shapes=[
                pltpu.VMEM((topk, tokens), jnp.int32),
                pltpu.VMEM((1, width), F32),
                pltpu.VMEM((tokens, width), BF16),
                pltpu.VMEM((tokens, width), BF16),
                pltpu.VMEM((tokens, width), BF16),
            ]
            + [pltpu.VMEM((rows, ends[1] - ends[0]), BF16) for ends in columns]
            + [
                pltpu.SemaphoreType.DMA((2, pieces)),
                pltpu.SemaphoreType.DMA((2,)),
                pltpu.SemaphoreType.DMA((chips * len(columns),)),
            ],
            compiler_params=params(mib),
            name="dispatch",
        )(late, me, ids, skip_gain, acts[0], skip_rows[0])

    sent = [*dispatch(incoming[:1], 62), *dispatch(incoming[1:], 24)]

    def hold(block):
        return pl.pallas_call(
            hold_kernel,
            out_shape=jax.ShapeDtypeStruct(block.shape, block.dtype),
            in_specs=[ANY],
            out_specs=VMEM,
            scratch_shapes=[pltpu.SemaphoreType.DMA],
            compiler_params=params(16),
            name="hold",
        )(block)

    other_first = hold(across_core(first))
    other_second = hold(across_core(second))

    mix, h_rows = pl.pallas_call(
        lambda *refs: gate_kernel(experts, slots, *refs),
        out_shape=(
            jax.ShapeDtypeStruct((tokens, rows), BF16),
            jax.ShapeDtypeStruct((tokens, width), F32),
        ),
        in_specs=[SMEM, SMEM] + [VMEM] * 5,
        out_specs=(VMEM, VMEM),
        compiler_params=params(16),
        name="gates",
    )(late, me, ids, skip_gain, acts[0], skip_rows[0], router[0].T)

    total = mix
    for c, ends in enumerate(incoming):
        arrived = exchange(sent[c * chips : (c + 1) * chips])
        last = c == len(incoming) - 1
        total = pl.pallas_call(
            lambda *refs, c=c, ends=ends, last=last: first_kernel(
                chips, slots, ends, min(512, hidden_width), c == 0, last, *refs
            ),
            out_shape=jax.ShapeDtypeStruct((rows, hidden_width), BF16 if last else F32),
            in_specs=[VMEM] * (chips + 2) + [ANY if c == 0 else VMEM, ANY],
            out_specs=VMEM,
            scratch_shapes=[pltpu.VMEM((2, chips * slots, ends[1] - ends[0]), BF16)],
            compiler_params=params(16),
            name="first_matmul",
        )(*arrived, first, other_first, total, mix if c == 0 else other_second)
    hidden = total

    mirror = [(s, sections - 1 - s) for s in range(sections)]
    same = [s for s in range(sections) if (s - 1) % sections == sections - 1 - s]
    onward = [((s - 1) % sections, s) for s in range(sections) if s not in same]
    shared = jnp.zeros((), jnp.bool_)
    for s in same:
        shared = shared | (section_pos == s)
    shared = shared.astype(jnp.int32).reshape(1)
    made, gone, placed = [], [], []
    for c, ends in enumerate(outgoing):
        after = gone[c - 2] + [made[c - 1]] if c >= 2 else []
        worked = pl.pallas_call(
            lambda *refs, ends=ends: second_kernel(chips, slots, ends, *refs),
            out_shape=sendable(ends),
            in_specs=[VMEM] * 3 + [ANY] * len(after),
            out_specs=[VMEM] * chips,
            compiler_params=params(16),
            name="second_matmul",
        )(hidden, second, other_second, *after)
        back = exchange(worked)
        y = pl.pallas_call(
            lambda *refs, ends=ends: combine_kernel(chips, ends, *refs),
            out_shape=jax.ShapeDtypeStruct((tokens, ends[1] - ends[0]), BF16),
            in_specs=[VMEM] * (chips + 2),
            out_specs=VMEM,
            scratch_shapes=[pltpu.VMEM((rows, ends[1] - ends[0]), BF16)],
            compiler_params=params(16),
            name="combine",
        )(h_rows, mix, *back)
        made.append(y)
        across = lax.ppermute(y, "section", mirror)
        ahead = lax.ppermute(y, "section", onward) if onward else across
        gone.append([across, ahead])
        placed = pl.pallas_call(
            lambda *refs, ends=ends: place_kernel(ends, *refs),
            out_shape=[jax.ShapeDtypeStruct((tokens, width), BF16)] * 2,
            in_specs=[SMEM, ANY, ANY] + [HBM] * len(placed),
            out_specs=[HBM, HBM],
            scratch_shapes=[pltpu.SemaphoreType.DMA((2,))],
            input_output_aliases={3: 0, 4: 1} if placed else {},
            compiler_params=params(16),
            name="place",
        )(shared, across, ahead, *placed)
    return (placed[0][None], placed[1][None])


def solution(mesh):
    placed = (
        P("section", "expert", None),
        P("section", "expert", None),
        P("section", None, None),
        P("section", None),
        P("section", "expert", None),
        P("section", "expert", None, None),
        P("section", "expert", None, None),
    )
    return jax.shard_map(
        local,
        mesh=mesh,
        in_specs=placed,
        out_specs=(P("section", "expert", None), P("section", "expert", None)),
        check_vma=False,
    )
```

```python
import jax
import jax.numpy as jnp
from jax import lax
from jax.experimental import pallas as pl
from jax.experimental.pallas import tpu as pltpu
from jax.sharding import PartitionSpec as P

VMEM = pl.BlockSpec(memory_space=pltpu.VMEM)
SMEM = pl.BlockSpec(memory_space=pltpu.SMEM)
HBM = pl.BlockSpec(memory_space=pltpu.HBM)
ANY = pl.BlockSpec(memory_space=pl.ANY)
BF16 = jnp.bfloat16
F32 = jnp.float32
IN_PARTS = (6, 8, 2)
OUT_PARTS = (5, 7, 4)


def cut(width, parts):
    unit, start, ranges = width // sum(parts), 0, []
    for part in parts:
        ranges.append((start, start + part * unit))
        start += part * unit
    return ranges


def inverse_rms(values):
    return lax.rsqrt(jnp.mean(values * values, axis=-1, keepdims=True) + 1e-06)


def matmul(a, b):
    return jnp.dot(a, b, preferred_element_type=F32)


def slot_table(me, ids, experts, slots):
    tokens = ids.shape[1]
    rows = experts * slots
    expert = lax.broadcasted_iota(jnp.int32, (experts, tokens), 0) ^ me
    named = jnp.zeros((experts, tokens), F32)
    for k in range(ids.shape[0]):
        named = named + jnp.where(ids[k : k + 1, :] == expert, 1.0, 0.0)
    before = lax.broadcasted_iota(jnp.int32, (tokens, tokens), 0)
    after = lax.broadcasted_iota(jnp.int32, (tokens, tokens), 1)
    earlier = jnp.where(before < after, 1.0, 0.0)
    tally = matmul(named.astype(BF16), earlier.astype(BF16))
    slot = jnp.where(named > 0.0, tally, -1.0)
    row = lax.broadcasted_iota(jnp.int32, (rows, experts), 0)
    low = lax.broadcasted_iota(jnp.int32, (rows, experts), 1) * slots
    spread = jnp.where((row >= low) & (row < low + slots), 1.0, 0.0)
    wanted = matmul(spread.astype(BF16), slot.astype(BF16))
    first = jnp.sum(spread * low.astype(F32), axis=1, keepdims=True)
    place = lax.broadcasted_iota(jnp.int32, (rows, 1), 0).astype(F32) - first
    return wanted == place, spread.astype(BF16), named, expert


def sum_rows(late, acts, skip, gain):
    skip = skip.astype(F32)
    term = gain * (skip * inverse_rms(skip))
    return acts.astype(F32) + jnp.where(late > 0, term, jnp.zeros_like(term))


def dispatch_kernel(experts, slots, pieces, columns, late_ref, me_ref, ids_hbm, gain_hbm, acts_hbm, skip_hbm, *rest):
    chips = experts // 2
    out_refs = rest[: chips * len(columns)]
    ids_ref, gain_ref, acts_ref, skip_ref, normed_ref, *held, sems, small, done = rest[chips * len(columns) :]
    tokens = acts_ref.shape[0]
    size = tokens // pieces
    ids_copy = pltpu.make_async_copy(ids_hbm, ids_ref, small.at[0])
    gain_copy = pltpu.make_async_copy(gain_hbm, gain_ref, small.at[1])
    ids_copy.start()
    gain_copy.start()
    copies = []
    for r in range(pieces):
        part = pl.ds(r * size, size)
        pair = (
            pltpu.make_async_copy(skip_hbm.at[part], skip_ref.at[part], sems.at[0, r]),
            pltpu.make_async_copy(acts_hbm.at[part], acts_ref.at[part], sems.at[1, r]),
        )
        for copy in pair:
            copy.start()
        copies.append(pair)
    ids_copy.wait()
    taken, _, _, _ = slot_table(me_ref[0], ids_ref[...], experts, slots)
    pick = jnp.where(taken, 1.0, 0.0).astype(BF16)
    gain_copy.wait()
    for r in range(pieces):
        part = pl.ds(r * size, size)
        for copy in copies[r]:
            copy.wait()
        h = sum_rows(late_ref[0], acts_ref[part], skip_ref[part], gain_ref[...])
        normed_ref[part] = (h * inverse_rms(h)).astype(BF16)
    sends = []
    for c, ends in enumerate(columns):
        held[c][...] = matmul(pick, normed_ref[:, ends[0] : ends[1]]).astype(BF16)
        for k in range(chips):
            block = held[c].at[pl.ds(k * 2 * slots, 2 * slots)]
            send = pltpu.make_async_copy(block, out_refs[c * chips + k], done.at[c * chips + k])
            send.start()
            sends.append(send)
    for send in sends:
        send.wait()


def gate_kernel(experts, slots, late_ref, me_ref, ids_ref, gain_ref, acts_ref, skip_ref, router_ref, mix_ref, h_ref):
    h = sum_rows(late_ref[0], acts_ref[...], skip_ref[...], gain_ref[...])
    h_ref[...] = h
    normed = (h * inverse_rms(h)).astype(BF16)
    logits = lax.dot_general(
        router_ref[...], normed, (((1,), (1,)), ((), ())), preferred_element_type=F32
    )
    taken, spread, named, expert = slot_table(me_ref[0], ids_ref[...], experts, slots)
    natural = lax.broadcasted_iota(jnp.int32, (experts, ids_ref.shape[1]), 0)
    chosen = jnp.zeros(natural.shape, F32)
    for k in range(ids_ref.shape[0]):
        chosen = chosen + jnp.where(ids_ref[k : k + 1, :] == natural, 1.0, 0.0)
    peak = jnp.max(jnp.where(chosen > 0.0, logits, -jnp.inf), axis=0, keepdims=True)
    mass = jnp.where(chosen > 0.0, jnp.exp(logits - peak), 0.0)
    gates = (mass / jnp.sum(mass, axis=0, keepdims=True)).astype(BF16)
    order = lax.broadcasted_iota(jnp.int32, (experts, experts), 0) ^ me_ref[0]
    swap = jnp.where(order == lax.broadcasted_iota(jnp.int32, (experts, experts), 1), 1.0, 0.0)
    turned = matmul(swap.astype(BF16), gates).astype(BF16)
    wide = matmul(spread, turned)
    mix_ref[...] = jnp.where(taken, wide, 0.0).T.astype(BF16)


def hold_kernel(source, target, sem):
    copy = pltpu.make_async_copy(source, target, sem)
    copy.start()
    copy.wait()


def first_kernel(chips, slots, columns, tile, first, last, *refs):
    blocks, (own_ref, other_ref, before_ref), (out_ref, held) = refs[:chips], refs[chips : chips + 3], refs[-2:]
    for k in range(chips):
        for half in range(2):
            held[half, k * slots : (k + 1) * slots] = blocks[k][half * slots : (half + 1) * slots]
    size = chips * slots
    for half, weight in enumerate((own_ref, other_ref)):
        part = slice(half * size, (half + 1) * size)
        for j in range(0, out_ref.shape[1], tile):
            total = matmul(held[half], weight[columns[0] : columns[1], j : j + tile])
            if not first:
                total = total + before_ref[part, j : j + tile]
            out_ref[part, j : j + tile] = jax.nn.gelu(total, approximate=True).astype(BF16) if last else total


def bridge_kernel(chips, slots, incoming, outgoing, tile, *refs):
    blocks, first_refs, second_refs = refs[:chips], refs[chips : chips + 3], refs[chips + 3 : chips + 5]
    hidden_ref, out_refs, held = refs[-chips - 2], refs[-chips - 1 : -1], refs[-1]
    first_kernel(chips, slots, incoming, tile, False, True, *blocks, *first_refs, hidden_ref, held)
    second_kernel(chips, slots, outgoing, hidden_ref, *second_refs, *out_refs)


def second_kernel(chips, slots, columns, hidden_ref, own_ref, other_ref, *refs):
    size = chips * slots
    out_refs = refs[-chips:]
    for half, weight in enumerate((own_ref, other_ref)):
        worked = matmul(hidden_ref[half * size : (half + 1) * size], weight[:, columns[0] : columns[1]]).astype(BF16)
        for k in range(chips):
            out_refs[k][half * slots : (half + 1) * slots] = worked[k * slots : (k + 1) * slots]


def combine_kernel(chips, columns, h_ref, mix_ref, *refs):
    blocks, out_ref, held = refs[:chips], refs[-2], refs[-1]
    size = blocks[0].shape[0]
    for k in range(chips):
        held[k * size : (k + 1) * size] = blocks[k][...]
    out_ref[...] = (h_ref[:, columns[0] : columns[1]] + matmul(mix_ref[...], held[...])).astype(BF16)


def place_kernel(columns, shared_ref, across_ref, onward_ref, *refs):
    handed_ref, mirrored_ref, sems = refs[-3:]
    part = pl.ds(columns[0], columns[1] - columns[0])
    copy = pltpu.make_async_copy(across_ref, mirrored_ref.at[:, part], sems.at[0])
    copy.start()

    @pl.when(shared_ref[0] > 0)
    def _():
        again = pltpu.make_async_copy(across_ref, handed_ref.at[:, part], sems.at[1])
        again.start()
        again.wait()

    @pl.when(shared_ref[0] == 0)
    def _():
        again = pltpu.make_async_copy(onward_ref, handed_ref.at[:, part], sems.at[1])
        again.start()
        again.wait()

    copy.wait()


def local(acts, expert_ids, router, skip_gain, skip_rows, w_in, w_out):
    section_pos = lax.axis_index("section")
    sections = lax.axis_size("section")
    devices = lax.axis_size("expert")
    tokens, width = acts.shape[1:]
    topk = expert_ids.shape[2]
    experts = router.shape[2]
    hidden_width = w_in.shape[3]
    capacity = 3 * tokens * topk // (2 * experts)
    slots = -(-capacity // 16) * 16
    rows = experts * slots
    chips = devices // 2

    def params(mib):
        return pltpu.CompilerParams(vmem_limit_bytes=mib * 2**20)

    late = (section_pos >= sections // 2).astype(jnp.int32).reshape(1)
    me = lax.axis_index("expert").astype(jnp.int32).reshape(1)
    ids = expert_ids[0].T
    first, second = w_in[0, 0], w_out[0, 0]

    def across_core(block):
        return lax.ppermute(block, "expert", [(i, i ^ 1) for i in range(devices)])

    def exchange(blocks):
        return [blocks[0]] + [
            lax.ppermute(blocks[k], "expert", [(i, i ^ (2 * k)) for i in range(devices)])
            for k in range(1, chips)
        ]

    incoming = cut(width, IN_PARTS)
    outgoing = cut(width, OUT_PARTS)

    def sendable(ends):
        return [jax.ShapeDtypeStruct((2 * slots, ends[1] - ends[0]), BF16)] * chips

    pieces = 2
    def dispatch(columns, mib):
        return pl.pallas_call(
            lambda *refs: dispatch_kernel(experts, slots, pieces, columns, *refs),
            out_shape=[shape for ends in columns for shape in sendable(ends)],
            in_specs=[SMEM, SMEM, HBM, HBM, HBM, HBM],
            out_specs=[HBM] * (chips * len(columns)),
            scratch_shapes=[
                pltpu.VMEM((topk, tokens), jnp.int32),
                pltpu.VMEM((1, width), F32),
                pltpu.VMEM((tokens, width), BF16),
                pltpu.VMEM((tokens, width), BF16),
                pltpu.VMEM((tokens, width), BF16),
            ]
            + [pltpu.VMEM((rows, ends[1] - ends[0]), BF16) for ends in columns]
            + [
                pltpu.SemaphoreType.DMA((2, pieces)),
                pltpu.SemaphoreType.DMA((2,)),
                pltpu.SemaphoreType.DMA((chips * len(columns),)),
            ],
            compiler_params=params(mib),
            name="dispatch",
        )(late, me, ids, skip_gain, acts[0], skip_rows[0])

    sent = [*dispatch(incoming[:1], 62), *dispatch(incoming[1:], 24)]

    def hold(block):
        return pl.pallas_call(
            hold_kernel,
            out_shape=jax.ShapeDtypeStruct(block.shape, block.dtype),
            in_specs=[ANY],
            out_specs=VMEM,
            scratch_shapes=[pltpu.SemaphoreType.DMA],
            compiler_params=params(16),
            name="hold",
        )(block)

    other_first = hold(across_core(first))
    other_second = hold(across_core(second))

    mix, h_rows = pl.pallas_call(
        lambda *refs: gate_kernel(experts, slots, *refs),
        out_shape=(
            jax.ShapeDtypeStruct((tokens, rows), BF16),
            jax.ShapeDtypeStruct((tokens, width), F32),
        ),
        in_specs=[SMEM, SMEM] + [VMEM] * 5,
        out_specs=(VMEM, VMEM),
        compiler_params=params(16),
        name="gates",
    )(late, me, ids, skip_gain, acts[0], skip_rows[0], router[0].T)

    total = mix
    for c, ends in enumerate(incoming):
        arrived = exchange(sent[c * chips : (c + 1) * chips])
        last = c == len(incoming) - 1
        tile = min(512, hidden_width)
        held = pltpu.VMEM((2, chips * slots, ends[1] - ends[0]), BF16)
        if last:
            hidden, *early = pl.pallas_call(
                lambda *refs, ends=ends: bridge_kernel(chips, slots, ends, outgoing[0], tile, *refs),
                out_shape=[jax.ShapeDtypeStruct((rows, hidden_width), BF16)] + sendable(outgoing[0]),
                in_specs=[VMEM] * (chips + 5),
                out_specs=[VMEM] * (chips + 1),
                scratch_shapes=[held],
                compiler_params=params(16),
                name="bridge",
            )(*arrived, first, other_first, total, second, other_second)
            continue
        total = pl.pallas_call(
            lambda *refs, c=c, ends=ends: first_kernel(chips, slots, ends, tile, c == 0, False, *refs),
            out_shape=jax.ShapeDtypeStruct((rows, hidden_width), F32),
            in_specs=[VMEM] * (chips + 2) + [ANY if c == 0 else VMEM, ANY],
            out_specs=VMEM,
            scratch_shapes=[held],
            compiler_params=params(16),
            name="first_matmul",
        )(*arrived, first, other_first, total, mix if c == 0 else other_second)

    mirror = [(s, sections - 1 - s) for s in range(sections)]
    same = [s for s in range(sections) if (s - 1) % sections == sections - 1 - s]
    onward = [((s - 1) % sections, s) for s in range(sections) if s not in same]
    shared = jnp.zeros((), jnp.bool_)
    for s in same:
        shared = shared | (section_pos == s)
    shared = shared.astype(jnp.int32).reshape(1)
    made, gone, placed = [], [], []
    for c, ends in enumerate(outgoing):
        after = gone[c - 2] + [made[c - 1]] if c >= 2 else []
        worked = early if c == 0 else pl.pallas_call(
            lambda *refs, ends=ends: second_kernel(chips, slots, ends, *refs),
            out_shape=sendable(ends),
            in_specs=[VMEM] * 3 + [ANY] * len(after),
            out_specs=[VMEM] * chips,
            compiler_params=params(16),
            name="second_matmul",
        )(hidden, second, other_second, *after)
        back = exchange(worked)
        y = pl.pallas_call(
            lambda *refs, ends=ends: combine_kernel(chips, ends, *refs),
            out_shape=jax.ShapeDtypeStruct((tokens, ends[1] - ends[0]), BF16),
            in_specs=[VMEM] * (chips + 2),
            out_specs=VMEM,
            scratch_shapes=[pltpu.VMEM((rows, ends[1] - ends[0]), BF16)],
            compiler_params=params(16),
            name="combine",
        )(h_rows, mix, *back)
        made.append(y)
        across = lax.ppermute(y, "section", mirror)
        ahead = lax.ppermute(y, "section", onward) if onward else across
        gone.append([across, ahead])
        placed = pl.pallas_call(
            lambda *refs, ends=ends: place_kernel(ends, *refs),
            out_shape=[jax.ShapeDtypeStruct((tokens, width), BF16)] * 2,
            in_specs=[SMEM, ANY, ANY] + [HBM] * len(placed),
            out_specs=[HBM, HBM],
            scratch_shapes=[pltpu.SemaphoreType.DMA((2,))],
            input_output_aliases={3: 0, 4: 1} if placed else {},
            compiler_params=params(16),
            name="place",
        )(shared, across, ahead, *placed)
    return (placed[0][None], placed[1][None])


def solution(mesh):
    placed = (
        P("section", "expert", None),
        P("section", "expert", None),
        P("section", None, None),
        P("section", None),
        P("section", "expert", None),
        P("section", "expert", None, None),
        P("section", "expert", None, None),
    )
    return jax.shard_map(
        local,
        mesh=mesh,
        in_specs=placed,
        out_specs=(P("section", "expert", None), P("section", "expert", None)),
        check_vma=False,
    )
```

```python
import jax
import jax.numpy as jnp
from jax import lax
from jax.experimental import pallas as pl
from jax.experimental.pallas import tpu as pltpu
from jax.sharding import PartitionSpec as P

VMEM = pl.BlockSpec(memory_space=pltpu.VMEM)
SMEM = pl.BlockSpec(memory_space=pltpu.SMEM)
HBM = pl.BlockSpec(memory_space=pltpu.HBM)
ANY = pl.BlockSpec(memory_space=pl.ANY)
BF16 = jnp.bfloat16
F32 = jnp.float32
IN_PARTS = (6, 8, 2)
OUT_PARTS = (5, 7, 4)


def cut(width, parts):
    unit, start, ranges = width // sum(parts), 0, []
    for part in parts:
        ranges.append((start, start + part * unit))
        start += part * unit
    return ranges


def inverse_rms(values):
    return lax.rsqrt(jnp.mean(values * values, axis=-1, keepdims=True) + 1e-06)


def matmul(a, b):
    return jnp.dot(a, b, preferred_element_type=F32)


def slot_table(me, ids, experts, slots):
    tokens = ids.shape[1]
    rows = experts * slots
    expert = lax.broadcasted_iota(jnp.int32, (experts, tokens), 0) ^ me
    named = jnp.zeros((experts, tokens), F32)
    for k in range(ids.shape[0]):
        named = named + jnp.where(ids[k : k + 1, :] == expert, 1.0, 0.0)
    before = lax.broadcasted_iota(jnp.int32, (tokens, tokens), 0)
    after = lax.broadcasted_iota(jnp.int32, (tokens, tokens), 1)
    earlier = jnp.where(before < after, 1.0, 0.0)
    tally = matmul(named.astype(BF16), earlier.astype(BF16))
    slot = jnp.where(named > 0.0, tally, -1.0)
    row = lax.broadcasted_iota(jnp.int32, (rows, experts), 0)
    low = lax.broadcasted_iota(jnp.int32, (rows, experts), 1) * slots
    spread = jnp.where((row >= low) & (row < low + slots), 1.0, 0.0)
    wanted = matmul(spread.astype(BF16), slot.astype(BF16))
    first = jnp.sum(spread * low.astype(F32), axis=1, keepdims=True)
    place = lax.broadcasted_iota(jnp.int32, (rows, 1), 0).astype(F32) - first
    return wanted == place, spread.astype(BF16), named, expert


def sum_rows(late, acts, skip, gain):
    skip = skip.astype(F32)
    term = gain * (skip * inverse_rms(skip))
    return acts.astype(F32) + jnp.where(late > 0, term, jnp.zeros_like(term))


def dispatch_kernel(experts, slots, pieces, columns, late_ref, me_ref, ids_hbm, gain_hbm, acts_hbm, skip_hbm, *rest):
    chips = experts // 2
    out_refs = rest[: chips * len(columns)]
    ids_ref, gain_ref, acts_ref, skip_ref, normed_ref, *held, sems, small, done = rest[chips * len(columns) :]
    tokens = acts_ref.shape[0]
    size = tokens // pieces
    ids_copy = pltpu.make_async_copy(ids_hbm, ids_ref, small.at[0])
    gain_copy = pltpu.make_async_copy(gain_hbm, gain_ref, small.at[1])
    ids_copy.start()
    gain_copy.start()
    copies = []
    for r in range(pieces):
        part = pl.ds(r * size, size)
        pair = (
            pltpu.make_async_copy(skip_hbm.at[part], skip_ref.at[part], sems.at[0, r]),
            pltpu.make_async_copy(acts_hbm.at[part], acts_ref.at[part], sems.at[1, r]),
        )
        for copy in pair:
            copy.start()
        copies.append(pair)
    ids_copy.wait()
    taken, _, _, _ = slot_table(me_ref[0], ids_ref[...], experts, slots)
    pick = jnp.where(taken, 1.0, 0.0).astype(BF16)
    gain_copy.wait()
    for r in range(pieces):
        part = pl.ds(r * size, size)
        for copy in copies[r]:
            copy.wait()
        h = sum_rows(late_ref[0], acts_ref[part], skip_ref[part], gain_ref[...])
        normed_ref[part] = (h * inverse_rms(h)).astype(BF16)
    sends = []
    for c, ends in enumerate(columns):
        held[c][...] = matmul(pick, normed_ref[:, ends[0] : ends[1]]).astype(BF16)
        for k in range(chips):
            block = held[c].at[pl.ds(k * 2 * slots, 2 * slots)]
            send = pltpu.make_async_copy(block, out_refs[c * chips + k], done.at[c * chips + k])
            send.start()
            sends.append(send)
    for send in sends:
        send.wait()


def gate_kernel(experts, slots, late_ref, me_ref, ids_ref, gain_ref, acts_ref, skip_ref, router_ref, mix_ref, h_ref):
    h = sum_rows(late_ref[0], acts_ref[...], skip_ref[...], gain_ref[...])
    h_ref[...] = h
    normed = (h * inverse_rms(h)).astype(BF16)
    logits = lax.dot_general(
        router_ref[...], normed, (((1,), (1,)), ((), ())), preferred_element_type=F32
    )
    taken, spread, named, expert = slot_table(me_ref[0], ids_ref[...], experts, slots)
    natural = lax.broadcasted_iota(jnp.int32, (experts, ids_ref.shape[1]), 0)
    chosen = jnp.zeros(natural.shape, F32)
    for k in range(ids_ref.shape[0]):
        chosen = chosen + jnp.where(ids_ref[k : k + 1, :] == natural, 1.0, 0.0)
    peak = jnp.max(jnp.where(chosen > 0.0, logits, -jnp.inf), axis=0, keepdims=True)
    mass = jnp.where(chosen > 0.0, jnp.exp(logits - peak), 0.0)
    gates = (mass / jnp.sum(mass, axis=0, keepdims=True)).astype(BF16)
    order = lax.broadcasted_iota(jnp.int32, (experts, experts), 0) ^ me_ref[0]
    swap = jnp.where(order == lax.broadcasted_iota(jnp.int32, (experts, experts), 1), 1.0, 0.0)
    turned = matmul(swap.astype(BF16), gates).astype(BF16)
    wide = matmul(spread, turned)
    mix_ref[...] = jnp.where(taken, wide, 0.0).T.astype(BF16)


def hold_kernel(source, target, sem):
    copy = pltpu.make_async_copy(source, target, sem)
    copy.start()
    copy.wait()


def first_kernel(chips, slots, columns, tile, first, last, *refs):
    blocks, (own_ref, other_ref, before_ref), (out_ref, held) = refs[:chips], refs[chips : chips + 3], refs[-2:]
    for k in range(chips):
        for half in range(2):
            held[half, k * slots : (k + 1) * slots] = blocks[k][half * slots : (half + 1) * slots]
    size = chips * slots
    for half, weight in enumerate((own_ref, other_ref)):
        part = slice(half * size, (half + 1) * size)
        for j in range(0, out_ref.shape[1], tile):
            total = matmul(held[half], weight[columns[0] : columns[1], j : j + tile])
            if not first:
                total = total + before_ref[part, j : j + tile]
            out_ref[part, j : j + tile] = jax.nn.gelu(total, approximate=True).astype(BF16) if last else total


def bridge_kernel(chips, slots, incoming, outgoing, tile, *refs):
    blocks, first_refs, second_refs = refs[:chips], refs[chips : chips + 3], refs[chips + 3 : chips + 5]
    hidden_ref, out_refs, held = refs[-chips - 2], refs[-chips - 1 : -1], refs[-1]
    first_kernel(chips, slots, incoming, tile, False, True, *blocks, *first_refs, hidden_ref, held)
    second_kernel(chips, slots, outgoing, hidden_ref, *second_refs, *out_refs)


def second_kernel(chips, slots, columns, hidden_ref, own_ref, other_ref, *refs):
    size = chips * slots
    out_refs = refs[-chips:]
    for half, weight in enumerate((own_ref, other_ref)):
        worked = matmul(hidden_ref[half * size : (half + 1) * size], weight[:, columns[0] : columns[1]]).astype(BF16)
        for k in range(chips):
            out_refs[k][half * slots : (half + 1) * slots] = worked[k * slots : (k + 1) * slots]


def combine_kernel(chips, columns, h_ref, mix_ref, *refs):
    blocks, out_ref, held = refs[:chips], refs[-2], refs[-1]
    size = blocks[0].shape[0]
    for k in range(chips):
        held[k * size : (k + 1) * size] = blocks[k][...]
    out_ref[...] = (h_ref[:, columns[0] : columns[1]] + matmul(mix_ref[...], held[...])).astype(BF16)


def place_kernel(columns, shared_ref, across_ref, onward_ref, *refs):
    handed_ref, mirrored_ref, sems = refs[-3:]
    part = pl.ds(columns[0], columns[1] - columns[0])
    copy = pltpu.make_async_copy(across_ref, mirrored_ref.at[:, part], sems.at[0])
    copy.start()

    @pl.when(shared_ref[0] > 0)
    def _():
        again = pltpu.make_async_copy(across_ref, handed_ref.at[:, part], sems.at[1])
        again.start()
        again.wait()

    @pl.when(shared_ref[0] == 0)
    def _():
        again = pltpu.make_async_copy(onward_ref, handed_ref.at[:, part], sems.at[1])
        again.start()
        again.wait()

    copy.wait()


def local(acts, expert_ids, router, skip_gain, skip_rows, w_in, w_out):
    section_pos = lax.axis_index("section")
    sections = lax.axis_size("section")
    devices = lax.axis_size("expert")
    tokens, width = acts.shape[1:]
    topk = expert_ids.shape[2]
    experts = router.shape[2]
    hidden_width = w_in.shape[3]
    capacity = 3 * tokens * topk // (2 * experts)
    slots = -(-capacity // 16) * 16
    rows = experts * slots
    chips = devices // 2

    def params(mib):
        return pltpu.CompilerParams(vmem_limit_bytes=mib * 2**20)

    late = (section_pos >= sections // 2).astype(jnp.int32).reshape(1)
    me = lax.axis_index("expert").astype(jnp.int32).reshape(1)
    ids = expert_ids[0].T
    first, second = w_in[0, 0], w_out[0, 0]

    def across_core(block):
        return lax.ppermute(block, "expert", [(i, i ^ 1) for i in range(devices)])

    def exchange(blocks):
        moved = {
            k: lax.ppermute(blocks[k], "expert", [(i, i ^ (2 * k)) for i in range(devices)])
            for k in range(chips - 1, 0, -1)
        }
        return [blocks[0]] + [moved[k] for k in range(1, chips)]

    incoming = cut(width, IN_PARTS)
    outgoing = cut(width, OUT_PARTS)

    def sendable(ends):
        return [jax.ShapeDtypeStruct((2 * slots, ends[1] - ends[0]), BF16)] * chips

    pieces = 2
    def dispatch(columns, mib):
        return pl.pallas_call(
            lambda *refs: dispatch_kernel(experts, slots, pieces, columns, *refs),
            out_shape=[shape for ends in columns for shape in sendable(ends)],
            in_specs=[SMEM, SMEM, HBM, HBM, HBM, HBM],
            out_specs=[HBM] * (chips * len(columns)),
            scratch_shapes=[
                pltpu.VMEM((topk, tokens), jnp.int32),
                pltpu.VMEM((1, width), F32),
                pltpu.VMEM((tokens, width), BF16),
                pltpu.VMEM((tokens, width), BF16),
                pltpu.VMEM((tokens, width), BF16),
            ]
            + [pltpu.VMEM((rows, ends[1] - ends[0]), BF16) for ends in columns]
            + [
                pltpu.SemaphoreType.DMA((2, pieces)),
                pltpu.SemaphoreType.DMA((2,)),
                pltpu.SemaphoreType.DMA((chips * len(columns),)),
            ],
            compiler_params=params(mib),
            name="dispatch",
        )(late, me, ids, skip_gain, acts[0], skip_rows[0])

    sent = [*dispatch(incoming[:1], 62), *dispatch(incoming[1:], 24)]

    def hold(block):
        return pl.pallas_call(
            hold_kernel,
            out_shape=jax.ShapeDtypeStruct(block.shape, block.dtype),
            in_specs=[ANY],
            out_specs=VMEM,
            scratch_shapes=[pltpu.SemaphoreType.DMA],
            compiler_params=params(16),
            name="hold",
        )(block)

    other_first = hold(across_core(first))
    other_second = hold(across_core(second))

    mix, h_rows = pl.pallas_call(
        lambda *refs: gate_kernel(experts, slots, *refs),
        out_shape=(
            jax.ShapeDtypeStruct((tokens, rows), BF16),
            jax.ShapeDtypeStruct((tokens, width), F32),
        ),
        in_specs=[SMEM, SMEM] + [VMEM] * 5,
        out_specs=(VMEM, VMEM),
        compiler_params=params(16),
        name="gates",
    )(late, me, ids, skip_gain, acts[0], skip_rows[0], router[0].T)

    total = mix
    for c, ends in enumerate(incoming):
        arrived = exchange(sent[c * chips : (c + 1) * chips])
        last = c == len(incoming) - 1
        tile = min(512, hidden_width)
        held = pltpu.VMEM((2, chips * slots, ends[1] - ends[0]), BF16)
        if last:
            hidden, *early = pl.pallas_call(
                lambda *refs, ends=ends: bridge_kernel(chips, slots, ends, outgoing[0], tile, *refs),
                out_shape=[jax.ShapeDtypeStruct((rows, hidden_width), BF16)] + sendable(outgoing[0]),
                in_specs=[VMEM] * (chips + 5),
                out_specs=[VMEM] * (chips + 1),
                scratch_shapes=[held],
                compiler_params=params(16),
                name="bridge",
            )(*arrived, first, other_first, total, second, other_second)
            continue
        total = pl.pallas_call(
            lambda *refs, c=c, ends=ends: first_kernel(chips, slots, ends, tile, c == 0, False, *refs),
            out_shape=jax.ShapeDtypeStruct((rows, hidden_width), F32),
            in_specs=[VMEM] * (chips + 2) + [ANY if c == 0 else VMEM, ANY],
            out_specs=VMEM,
            scratch_shapes=[held],
            compiler_params=params(16),
            name="first_matmul",
        )(*arrived, first, other_first, total, mix if c == 0 else other_second)

    mirror = [(s, sections - 1 - s) for s in range(sections)]
    same = [s for s in range(sections) if (s - 1) % sections == sections - 1 - s]
    onward = [((s - 1) % sections, s) for s in range(sections) if s not in same]
    shared = jnp.zeros((), jnp.bool_)
    for s in same:
        shared = shared | (section_pos == s)
    shared = shared.astype(jnp.int32).reshape(1)
    made, gone, placed = [], [], []
    for c, ends in enumerate(outgoing):
        after = gone[c - 2] + [made[c - 1]] if c >= 2 else []
        worked = early if c == 0 else pl.pallas_call(
            lambda *refs, ends=ends: second_kernel(chips, slots, ends, *refs),
            out_shape=sendable(ends),
            in_specs=[VMEM] * 3 + [ANY] * len(after),
            out_specs=[VMEM] * chips,
            compiler_params=params(16),
            name="second_matmul",
        )(hidden, second, other_second, *after)
        back = exchange(worked)
        y = pl.pallas_call(
            lambda *refs, ends=ends: combine_kernel(chips, ends, *refs),
            out_shape=jax.ShapeDtypeStruct((tokens, ends[1] - ends[0]), BF16),
            in_specs=[VMEM] * (chips + 2),
            out_specs=VMEM,
            scratch_shapes=[pltpu.VMEM((rows, ends[1] - ends[0]), BF16)],
            compiler_params=params(16),
            name="combine",
        )(h_rows, mix, *back)
        made.append(y)
        across = lax.ppermute(y, "section", mirror)
        ahead = lax.ppermute(y, "section", onward) if onward else across
        gone.append([across, ahead])
        placed = pl.pallas_call(
            lambda *refs, ends=ends: place_kernel(ends, *refs),
            out_shape=[jax.ShapeDtypeStruct((tokens, width), BF16)] * 2,
            in_specs=[SMEM, ANY, ANY] + [HBM] * len(placed),
            out_specs=[HBM, HBM],
            scratch_shapes=[pltpu.SemaphoreType.DMA((2,))],
            input_output_aliases={3: 0, 4: 1} if placed else {},
            compiler_params=params(16),
            name="place",
        )(shared, across, ahead, *placed)
    return (placed[0][None], placed[1][None])


def solution(mesh):
    placed = (
        P("section", "expert", None),
        P("section", "expert", None),
        P("section", None, None),
        P("section", None),
        P("section", "expert", None),
        P("section", "expert", None, None),
        P("section", "expert", None, None),
    )
    return jax.shard_map(
        local,
        mesh=mesh,
        in_specs=placed,
        out_specs=(P("section", "expert", None), P("section", "expert", None)),
        check_vma=False,
    )
```
